32 devices in a mesh: grp: 2 (over y), row: 4 (over x, core), col: 4 (over z).
Axes of the slice: x: 2, y: 2, z: 4, core: 2. Of those that a mesh axis runs over, the one named last changes fastest.
Arguments:
- counts: int32 [16384, 32768], P(('grp', 'row'), 'col'), parts along dimension 0, may hold values from 0 to 255, as said below
- ctx_counts: int32 [65536], P(('grp', 'col')), parts along dimension 0, may hold values from 1000 to 119531
- omega: bfloat16 [32768, 512], P('col'), may hold values from -6 to 6
Outputs:
- basis: float32 [16384, 512], P(('grp', 'row', 'col')), parts along dimension 0
- projected: float32 [65536, 512], P(('grp', 'col'), 'row'), parts along dimension 0
The draws below stay inside these ranges and needn't reach their ends.
There are 2 independent parts, one for each index of `grp`. The reference program is written for one: setup_inputs(seed, part) draws one part's arguments, and reference() takes and returns one part's arrays. A program takes and returns all parts, laid end to end along the dimension named above; an argument that names none is the same for every part. Nothing has to cross between parts.
Inputs may be any that keep to these rules, and one draw needn't show every extreme that they name: `counts`: every slab row has at least one positive count.
All inputs are finite; a program needn't handle non-finite values.
Results may differ from the reference program's by a relative error of at most 0.008.
Values may be sent and summed in bfloat16 or wider, within the bound.
No kernel may reach another device: no remote copies, remote signals or barrier semaphores. Data moves between devices by JAX's collectives and lax.ppermute only.
A program may use at most 256 MiB of HBM per device.

```python
import jax
import jax.numpy as jnp
from jax import lax

V = 32768
K = 512
R = 2048
SLAB = 8192
N_ROW = 4


def draw_counts(key, part):
    key = jax.random.fold_in(key, 11)
    key_rows, key_cols, key_vals = jax.random.split(key, 3)
    row_high = jax.random.randint(key_rows, (SLAB,), 4, 33)
    col_high = jax.random.randint(key_cols, (V,), 4, 33)
    row_high = row_high.at[0].set(32)
    col_high = col_high.at[V - 1].set(32)
    column = jnp.arange(V, dtype=jnp.int32)
    rowpos = jnp.arange(SLAB, dtype=jnp.int32)
    top = row_high[:, None] * col_high[None, :] * (V + 3 * column)[None, :] // (16 * V) + 1
    values = jax.random.randint(key_vals, (SLAB, V), 0, top)
    values = values.at[0, V - 1].set(top[0, V - 1] - 1)
    placed = column[None, :] == rowpos[:, None] * 7919 % V
    extra = jnp.logical_and(placed, values == 0).astype(jnp.int32)
    return values + extra


def draw_ctx_counts(key, part):
    key = jax.random.fold_in(key, 12)
    base = jax.random.randint(key, (V,), 1000, 30001)
    base = base.at[0].set(1000)
    base = base.at[V - 1].set(30000)
    column = jnp.arange(V, dtype=jnp.int32)
    return base * (64 + 192 * column // V) // 64


def block_levels(key, dims, cuts, low, top_value):
    def one(axis_at, parts):
        heights = jax.random.uniform(jax.random.fold_in(jax.random.fold_in(key, 6), axis_at), (parts,), jnp.float32, low / len(cuts), top_value / len(cuts))
        return jnp.repeat(jnp.exp(heights), dims[axis_at] // parts).reshape((-1,) + (1,) * (len(dims) - axis_at - 1))

    gain = one(*cuts[0])
    for cut in cuts[1:]:
        gain = gain * one(*cut)
    return gain


def scatter_about(key, dims, scale, reach, cuts=(), held_as=jnp.bfloat16):
    entries = scale * jax.random.normal(key, dims, jnp.float32)
    if cuts:
        entries = entries * block_levels(key, dims, cuts, -0.22, 0.18)
    return jnp.clip(entries, -reach, reach).astype(held_as)


def setup_inputs(seed: int = 0, part: int = 0) -> dict:
    keys = jax.random.split(jax.random.key(seed), 4)
    own_keys = jax.random.split(jax.random.fold_in(keys[3], part), 4)
    return {
        "counts": draw_counts(jax.random.fold_in(jax.random.fold_in(keys[3], part), 71), part),
        "ctx_counts": draw_ctx_counts(jax.random.fold_in(jax.random.fold_in(keys[3], part), 71), part),
        "omega": scatter_about(keys[2], (V, K), 1.0, 6.0, ((0, 4),)),
    }


def ppmi_block(block, row_total, log_ctx, log_total):
    safe = jnp.maximum(block, 1).astype(jnp.float32)
    value = jnp.log(safe) + log_total - jnp.log(row_total)[:, None] - log_ctx[None, :] - jnp.log(jnp.float32(5.0))
    return jnp.where(block > 0, jnp.maximum(value, 0.0), 0.0).astype(jnp.bfloat16)

def shift_gram(gram):
    size = gram.shape[0]
    amount = jnp.float32(0.0001) * jnp.trace(gram) / jnp.float32(size)
    return gram + amount * jnp.eye(size, dtype=jnp.float32)

def reference(counts, ctx_counts, omega):
    ctx_weight = ctx_counts.astype(jnp.float32) ** 0.75
    log_ctx = jnp.log(ctx_weight)
    log_total = jnp.log(jnp.sum(ctx_weight))
    blocks = counts.reshape(N_ROW, R, V)

    def sketch_block(block):
        row_total = lax.optimization_barrier(jnp.sum(block.astype(jnp.float32), axis=1))
        weights = ppmi_block(block, row_total, log_ctx, log_total)
        return (jnp.dot(weights.astype(jnp.float32), omega.astype(jnp.float32), preferred_element_type=jnp.float32), row_total)
    pieces, totals = lax.map(sketch_block, blocks)
    sketch = pieces.reshape(SLAB, K)
    gram = lax.dot_general(sketch, sketch, (((0,), (0,)), ((), ())), precision=lax.Precision.HIGHEST)
    lower = jnp.linalg.cholesky(shift_gram(gram))
    basis = lax.linalg.triangular_solve(lower, sketch, left_side=False, lower=True, transpose_a=True)
    basis_b = basis.astype(jnp.bfloat16).reshape(N_ROW, R, K)

    def add_block(total, items):
        block, row_total, rows_b = items
        weights = ppmi_block(block, row_total, log_ctx, log_total)
        term = lax.dot_general(weights.astype(jnp.float32), rows_b.astype(jnp.float32), (((0,), (0,)), ((), ())), preferred_element_type=jnp.float32)
        return (total + term, None)
    start = jnp.zeros((V, K), jnp.float32)
    total, unused = lax.scan(add_block, start, (blocks, totals, basis_b))
    projected = total / jnp.sqrt(jnp.float32(SLAB))
    return (basis, projected)
```

```python
import functools

import jax
import jax.numpy as jnp
from jax import lax
from jax.experimental import pallas as pl
from jax.experimental.pallas import tpu as pltpu
from jax.sharding import PartitionSpec as P

HIGHEST = lax.Precision.HIGHEST
F32 = jnp.float32
BF16 = jnp.bfloat16
NB = 128
ROWS = ((0,), (0,))
COLS = ((1,), (1,))
VMEM = pl.BlockSpec(memory_space=pltpu.VMEM)
SMEM = pl.BlockSpec(memory_space=pltpu.SMEM)
ANY = pl.BlockSpec(memory_space=pl.ANY)


def limit(mib):
    return pltpu.CompilerParams(vmem_limit_bytes=mib * 1024 * 1024)


def cost(flops, nbytes):
    return pl.CostEstimate(flops=int(flops), bytes_accessed=int(nbytes), transcendentals=0)


def dot(a, b, contract, precision=None):
    return lax.dot_general(a, b, (contract, ((), ())), precision=precision, preferred_element_type=F32)


def eye(n):
    return lax.broadcasted_iota(jnp.int32, (n, n), 0) == lax.broadcasted_iota(jnp.int32, (n, n), 1)


def totals_body(order, counts, token, out):
    tile, width = counts.shape
    acc = counts[:, 0:NB]
    for c in range(NB, width, NB):
        acc = acc + counts[:, c : c + NB]
    column = jnp.sum(acc.astype(F32), axis=1, keepdims=True)
    out[0] = jnp.sum(jnp.where(eye(tile), column, 0.0), axis=0, keepdims=True)


def row_sums(counts, order, token, k, tile, n_chunk):
    n = order.shape[0]
    width = counts.shape[1]
    return pl.pallas_call(
        totals_body,
        grid_spec=pltpu.PrefetchScalarGridSpec(
            num_scalar_prefetch=1,
            grid=(n,),
            in_specs=[pl.BlockSpec((tile, width), lambda g, o: (o[g] * n_chunk + k, 0)), ANY],
            out_specs=pl.BlockSpec((1, 1, tile), lambda g, o: (g, 0, 0)),
        ),
        out_shape=jax.ShapeDtypeStruct((n, 1, tile), F32),
        name="row_sums",
        cost_estimate=cost(n * tile * width, 4 * n * tile * width),
        compiler_params=limit(32),
    )(order, counts, token)


def weigh_body(order, counts, base, log_ctx, omega, *refs):
    w, send, own = refs[-3:]
    tile, width = counts.shape
    column = jnp.sum(jnp.where(eye(tile), base[0], 0.0), axis=1, keepdims=True)
    step = 1024
    acc = jnp.zeros(own.shape, F32)
    for c in range(0, width, step):
        here = slice(c, c + step)
        for r in range(0, tile, 16):
            rows = slice(r, r + 16)
            value = jnp.log(counts[rows, here].astype(F32)) + (column[rows] - log_ctx[:, here])
            w[rows, here] = jnp.maximum(value, 0.0).astype(BF16)
        acc = acc + jnp.dot(w[:, here], omega[here, :], preferred_element_type=F32)
    send[0] = acc.astype(BF16)
    own[...] = acc


def weigh(counts, base, log_ctx, omega, w, order, k, tile, n_chunk):
    n = order.shape[0]
    rows, width = counts.shape
    size = omega.shape[1]
    place = lambda g, o: (o[g] * n_chunk + k, 0)
    held = [] if w is None else [w]
    return pl.pallas_call(
        weigh_body,
        grid_spec=pltpu.PrefetchScalarGridSpec(
            num_scalar_prefetch=1,
            grid=(n,),
            in_specs=[
                pl.BlockSpec((tile, width), place),
                pl.BlockSpec((1, 1, tile), lambda g, o: (g, 0, 0)),
                pl.BlockSpec((1, width), lambda g, o: (0, 0)),
                pl.BlockSpec((width, size), lambda g, o: (0, 0), pipeline_mode=pl.Buffered(1)),
            ]
            + [ANY] * len(held),
            out_specs=[
                pl.BlockSpec((tile, width), place),
                pl.BlockSpec((1, tile, size), lambda g, o: (g, 0, 0)),
                pl.BlockSpec((tile, size), lambda g, o: (0, 0)),
            ],
        ),
        out_shape=[
            jax.ShapeDtypeStruct((rows, width), BF16),
            jax.ShapeDtypeStruct((n, tile, size), BF16),
            jax.ShapeDtypeStruct((tile, size), F32),
        ],
        input_output_aliases={5: 0} if held else {},
        name="weigh_and_sketch",
        cost_estimate=cost(2 * n * tile * width * size, 6 * n * tile * width),
        compiler_params=limit(44),
    )(order, counts, base, log_ctx, omega, *held)


PACKED = (((0, 0), (0, 1), (0, 2), (0, 3), (3, 3)), ((1, 1), (1, 2), (1, 3), (2, 2), (2, 3)))


def gram_body(n_chunk, n_part, *refs):
    parts, (sketch, sketch_b, packed) = refs[:-3], refs[-3:]
    tile = parts[0].shape[0]
    for k in range(n_chunk):
        mine = parts[k * n_part : (k + 1) * n_part]
        total = mine[0][...]
        for other in mine[1:]:
            total = total + other[...].astype(F32)
        sketch[k * tile : (k + 1) * tile, :] = total
    sketch_b[...] = sketch[...].astype(BF16)
    size = sketch.shape[1] // 4
    col = lambda i, j: sketch[:, i * size : j * size]
    for i, j, half, at in ((0, 4, 0, 0), (3, 4, 0, 4), (1, 4, 1, 0), (2, 4, 1, 3)):
        packed[half * size : (half + 1) * size, at * size : (at + j - i) * size] = dot(
            col(i, i + 1), col(i, j), ROWS, HIGHEST
        )


def gram_of(parts, n_chunk, n_part):
    tile, size = parts[0].shape
    rows = tile * n_chunk
    return pl.pallas_call(
        functools.partial(gram_body, n_chunk, n_part),
        in_specs=[VMEM] * len(parts),
        out_specs=[VMEM] * 3,
        out_shape=[
            jax.ShapeDtypeStruct((rows, size), F32),
            jax.ShapeDtypeStruct((rows, size), BF16),
            jax.ShapeDtypeStruct((size // 2, size // 4 * 5), F32),
        ],
        name="gram",
        cost_estimate=cost(12 * rows * size * size, 8 * rows * size),
        compiler_params=limit(32),
    )(*parts)


def eliminate(tiles):
    shape = tiles[0].shape
    lane = lax.broadcasted_iota(jnp.int32, shape, 1)
    sub = lax.broadcasted_iota(jnp.int32, shape, 0)
    spread = lambda x: jnp.broadcast_to(x, shape)
    tiles = list(tiles)
    for j in range(0, NB, 2):
        t, s = divmod(j, 8)
        first = {i: spread(tiles[i][:, j : j + 1]) for i in range(t, len(tiles))}
        second = {i: spread(tiles[i][:, j + 1 : j + 2]) for i in range(t, len(tiles))}
        a = spread(first[t][s : s + 1])
        b = spread(first[t][s + 1 : s + 2])
        c = spread(second[t][s + 1 : s + 2])
        at_first, at_second = lane == j, lane == j + 1
        pair = at_first | at_second
        row_a = jnp.where(pair, jnp.where(at_first, 1.0, 0.0), spread(tiles[t][s : s + 1]))
        row_b = jnp.where(pair, jnp.where(at_second, 1.0, 0.0), spread(tiles[t][s + 1 : s + 2]))
        over = 1.0 / (a * c - b * b)
        use_a = (c * row_a - b * row_b) * over
        use_b = (a * row_b - b * row_a) * over
        done_a = row_a * lax.rsqrt(a)
        done_b = use_b * lax.rsqrt(a * over)
        for i in range(t, len(tiles)):
            new = jnp.where(pair, 0.0, tiles[i]) - first[i] * use_a - second[i] * use_b
            if i == t:
                kept = jnp.where(sub == s, done_a, jnp.where(sub == s + 1, done_b, tiles[i]))
                new = jnp.where(sub > s + 1, new, kept)
            tiles[i] = new
    return tiles


def factor_body(core, mine, other, out, halves, t):
    size = t.shape[0]
    n = size // NB
    block = lambda i: slice(i * NB, (i + 1) * NB)
    halves[core[0]] = mine[...]
    halves[1 - core[0]] = other[...]
    trace = jnp.float32(0.0)
    for half in range(2):
        for at, (i, j) in enumerate(PACKED[half]):
            value = halves[half, :, block(at)]
            t[block(i), block(j)] = value
            if i == j:
                trace = trace + jnp.sum(jnp.where(eye(NB), value, 0.0))
    amount = jnp.float32(0.0001) * trace / jnp.float32(size)
    lower = lax.broadcasted_iota(jnp.int32, (NB, NB), 1) <= lax.broadcasted_iota(jnp.int32, (NB, NB), 0)
    for p in range(n):
        here, before = block(p), slice(0, p * NB)
        diagonal = t[here, here] + jnp.where(eye(NB), amount, 0.0)
        tiles = eliminate([diagonal[8 * i : 8 * i + 8] for i in range(NB // 8)])
        inverse = jnp.where(lower, jnp.concatenate(tiles, 0), 0.0)
        out[here, here] = inverse
        if p:
            left = dot(inverse, t[here, before], ((1,), (0,)), HIGHEST)
            out[here, before] = left
        if p < n - 1:
            rest = slice((p + 1) * NB, size)
            out[here, rest] = jnp.zeros((NB, size - (p + 1) * NB), F32)
            right = dot(inverse, t[here, rest], ((1,), (0,)), HIGHEST)
            for q in range(p + 1, n):
                off = (q - p - 1) * NB
                use = right[:, off : off + NB]
                t[block(q), q * NB :] = t[block(q), q * NB :] - dot(use, right[:, off:], ROWS, HIGHEST)
                t[block(q), here] = -dot(use, inverse, ROWS, HIGHEST)
                if p:
                    t[block(q), before] = t[block(q), before] - dot(use, left, ROWS, HIGHEST)


def factor_inverse(core, mine, other):
    size = mine.shape[0] * 4
    return pl.pallas_call(
        factor_body,
        in_specs=[SMEM, VMEM, VMEM],
        out_specs=VMEM,
        out_shape=jax.ShapeDtypeStruct((size, size), F32),
        scratch_shapes=[pltpu.VMEM((2,) + mine.shape, F32), pltpu.VMEM((size, size), F32)],
        name="factor_inverse",
        cost_estimate=cost(2 * size**3 * 20, 8 * size * size),
        compiler_params=limit(32),
    )(core, mine, other)


def basis_body(place, inverse, sketch, *refs):
    shares, (basis, turned) = refs[:-2], refs[-2:]
    n = len(shares)
    rows, size = sketch.shape
    quarter = size // 4
    basis[...] = dot(sketch[...], inverse[...], COLS, HIGHEST)
    for i in range(4):
        take = inverse[pl.ds(pl.multiple_of(place[i] * quarter, quarter), quarter), :]
        high = take.astype(BF16)
        low = (take - high.astype(F32)).astype(BF16)
        for d in range(n):
            width = shares[d].shape[0]
            start = pl.multiple_of(place[4 + d] * width, width)
            value = dot(high, shares[d][...], COLS) + dot(low, shares[d][...], COLS)
            turned[i * quarter : (i + 1) * quarter, pl.ds(start, width)] = value.astype(BF16)


def basis_of(place, inverse, sketch, shares):
    rows, size = sketch.shape
    n = len(shares)
    return pl.pallas_call(
        basis_body,
        in_specs=[SMEM] + [VMEM] * (2 + n),
        out_specs=[VMEM] * 2,
        out_shape=[
            jax.ShapeDtypeStruct((rows, size), F32),
            jax.ShapeDtypeStruct((size, n * shares[0].shape[0]), BF16),
        ],
        name="basis",
        cost_estimate=cost(2 * rows * size * size * (6 + 2 * n), 4 * rows * size * (2 + n)),
        compiler_params=limit(32),
    )(place, inverse, sketch, *shares)


def project_body(turned, w, send, own):
    half = send.shape[0]
    value = jnp.dot(turned[...], w[...], preferred_element_type=F32)
    send[...] = value[:half].astype(BF16)
    own[...] = value[half:]


def project(turned, w, j, width, tile):
    size, rows = turned.shape
    steps = width // tile
    out = lambda g: (0, g)
    return pl.pallas_call(
        project_body,
        grid=(steps,),
        in_specs=[
            pl.BlockSpec((size, rows), lambda g: (0, 0), pipeline_mode=pl.Buffered(1)),
            pl.BlockSpec((rows, tile), lambda g: (0, j * steps + g)),
        ],
        out_specs=[pl.BlockSpec((size // 2, tile), out), pl.BlockSpec((size // 2, tile), out)],
        out_shape=[
            jax.ShapeDtypeStruct((size // 2, width), BF16),
            jax.ShapeDtypeStruct((size // 2, width), F32),
        ],
        name="project",
        cost_estimate=cost(2 * rows * size * width, 2 * rows * width),
        compiler_params=limit(32),
    )(turned, w)


def finish_body(scale, mine, core_term, chip_term, *refs):
    total = mine[...] + core_term[...].astype(F32) + chip_term[...].astype(F32)
    refs[-1][...] = jnp.transpose(total * scale)


def finish(own, core_term, chip_term, out, j, n_piece, scale):
    size, width = chip_term.shape
    held = [] if out is None else [out]
    return pl.pallas_call(
        functools.partial(finish_body, scale),
        grid=(1,),
        in_specs=[
            pl.BlockSpec((size, width), lambda g: (1, 0)),
            pl.BlockSpec((size, width), lambda g: (1, 0)),
            pl.BlockSpec((size, width), lambda g: (0, 0)),
        ]
        + [ANY] * len(held),
        out_specs=pl.BlockSpec((width, size), lambda g: (j, 0)),
        out_shape=jax.ShapeDtypeStruct((width * n_piece, size), F32),
        input_output_aliases={3: 0} if held else {},
        name="finish",
        cost_estimate=cost(size * width, 14 * size * width),
        compiler_params=limit(32),
    )(own, core_term, chip_term, *held)


def rotate(x, n, by):
    return lax.ppermute(x, "col", [(i, (i + by) % n) for i in range(n)])


def swap(x, bit):
    return lax.ppermute(x, "row", [(i, i ^ bit) for i in range(4)])


def half_of(x, which):
    rows = x.shape[0] // 2
    return lax.dynamic_slice_in_dim(x, which * rows, rows, 0)


def stack_by(which, mine, other):
    return jnp.where(which == 0, jnp.concatenate([mine, other]), jnp.concatenate([other, mine]))


def sketch_phase(counts, log_ctx, ctx_sum, omega):
    rows, width = counts.shape
    n = lax.axis_size("col")
    me = lax.axis_index("col")
    tile = NB
    n_chunk = rows // n // tile
    order = (me + 1 + jnp.arange(n, dtype=jnp.int32)) % n
    w = None
    sums = {}
    log_total = None

    def start_sums(k, token):
        part = row_sums(counts, order, token, k, tile, n_chunk)
        if k == 0:
            part = jnp.concatenate([part, jnp.broadcast_to(ctx_sum, (1, 1, tile))])
        sums[k] = part

    def total(k):
        mine = sums[k]
        whole = mine[:n]
        for d in range(1, n):
            got = rotate(mine, n, d)
            whole = whole + jnp.roll(got[:n], -d, axis=0)
            if k == 0:
                mine_ctx.append(got[n, 0, 0])
        return whole

    mine_ctx = []
    ctx_dummy = ctx_sum.reshape(1, 1)
    start_sums(0, ctx_dummy)
    if n_chunk > 1:
        start_sums(1, sums[0])
    parts = []
    for k in range(n_chunk):
        row_total = total(k)
        if k == 0:
            log_total = jnp.log(ctx_sum + sum(mine_ctx)) - jnp.log(F32(5.0))
        base = log_total - jnp.log(row_total)
        w, send, own = weigh(counts, base, log_ctx, omega, w, order, k, tile, n_chunk)
        parts.append(own)
        parts += [rotate(send[d], n, d + 1) for d in range(n - 1)]
        if k + 2 < n_chunk:
            start_sums(k + 2, send)
    return w, parts, n_chunk


def sketch_phase_any(counts, log_ctx, ctx_sum, omega):
    row_part = jnp.sum(counts.astype(F32), axis=1)
    row_total, ctx_total = lax.psum((row_part, ctx_sum), "col")
    value = jnp.log(counts.astype(F32)) + (
        jnp.log(ctx_total) - jnp.log(F32(5.0)) - jnp.log(row_total)[:, None] - log_ctx
    )
    w = jnp.maximum(value, 0.0).astype(BF16)
    partial = jnp.dot(w, omega, preferred_element_type=F32)
    return w, [lax.psum_scatter(partial, "col", scatter_dimension=0, tiled=True)], 1


def shards(counts, ctx_counts, omega):
    rows, width = counts.shape
    n = lax.axis_size("col")
    row = lax.axis_index("row")
    col = lax.axis_index("col")
    core, chip = row % 2, row // 2
    ctx_weight = ctx_counts.astype(F32) ** 0.75
    ctx_sum = jnp.sum(ctx_weight)
    log_ctx = jnp.log(ctx_weight)[None, :]
    ring = n == 4 and rows % (n * NB) == 0
    phase = sketch_phase if ring else sketch_phase_any
    w, parts, n_chunk = phase(counts, log_ctx, ctx_sum, omega)
    sketch, sketch_b, packed = gram_of(parts, n_chunk, len(parts) // n_chunk)
    half = half_of(packed, core) + swap(half_of(packed, 1 - core), 1)
    quarter = half_of(half, chip) + swap(half_of(half, 1 - chip), 2)
    if ring:
        quarter = sum([rotate(quarter, n, d) for d in range(1, n)], quarter)
        shares = [sketch_b] + [rotate(sketch_b, n, d) for d in range(1, n)]
    else:
        quarter = lax.psum(quarter, "col")
        shares = [lax.all_gather(sketch_b, "col", tiled=True)]
    half = stack_by(chip, quarter, swap(quarter, 2))
    inverse = factor_inverse(core.reshape(1), half, swap(half, 1))
    held_from = [(col - d) % n for d in range(n)] if ring else [jnp.int32(0)]
    place = jnp.stack([row ^ 3, row ^ 1, row ^ 2, row] + held_from)
    basis, turned = basis_of(place, inverse, sketch, shares)
    n_piece = 8
    piece = width // n_piece
    scale = float(1.0 / (rows * lax.axis_size("row")) ** 0.5)
    size = omega.shape[1]
    out = None
    for j in range(n_piece):
        send, own = project(turned, w, j, piece, min(512, piece))
        core_term = swap(send, 1)
        chip_send = (own[: size // 4] + core_term[: size // 4].astype(F32)).astype(BF16)
        out = finish(own, core_term, swap(chip_send, 2), out, j, n_piece, scale)
    return (basis, out)


def solution(mesh):
    in_specs = (P(("grp", "row"), "col"), P(("grp", "col")), P("col", None))
    out_specs = (P(("grp", "row", "col"), None), P(("grp", "col"), "row"))
    return jax.shard_map(shards, mesh=mesh, in_specs=in_specs, out_specs=out_specs, check_vma=False)
```

```python
import functools

import jax
import jax.numpy as jnp
from jax import lax
from jax.experimental import pallas as pl
from jax.experimental.pallas import tpu as pltpu
from jax.sharding import PartitionSpec as P

HIGHEST = lax.Precision.HIGHEST
F32 = jnp.float32
BF16 = jnp.bfloat16
NB = 128
ROWS = ((0,), (0,))
COLS = ((1,), (1,))
VMEM = pl.BlockSpec(memory_space=pltpu.VMEM)
SMEM = pl.BlockSpec(memory_space=pltpu.SMEM)
ANY = pl.BlockSpec(memory_space=pl.ANY)
HBM = pl.BlockSpec(memory_space=pltpu.HBM)


def limit(mib):
    return pltpu.CompilerParams(vmem_limit_bytes=mib * 1024 * 1024)


def cost(flops, nbytes):
    return pl.CostEstimate(flops=int(flops), bytes_accessed=int(nbytes), transcendentals=0)


def whole(*shape):
    return pl.BlockSpec(shape, lambda *_: (0,) * len(shape))


def dot(a, b, contract, precision=None):
    return lax.dot_general(a, b, (contract, ((), ())), precision=precision, preferred_element_type=F32)


def eye(n):
    return lax.broadcasted_iota(jnp.int32, (n, n), 0) == lax.broadcasted_iota(jnp.int32, (n, n), 1)


def totals_body(counts, out, small):
    tile, width = counts.shape
    for at in range(tile // NB):
        parts = []
        for r in range(at * NB, (at + 1) * NB, 32):
            acc = None
            for c in range(0, width, NB):
                value = counts[r : r + 32, c : c + NB]
                small[r : r + 32, c : c + NB] = (value - 128).astype(jnp.int8)
                acc = value if acc is None else acc + value
            parts.append(jnp.sum(acc.astype(F32), axis=1, keepdims=True))
        column = jnp.concatenate(parts, 0)
        out[at] = jnp.sum(jnp.where(eye(NB), column, 0.0), axis=0, keepdims=True)


def row_sums(counts):
    rows, width = counts.shape
    tile = 2 * NB
    return pl.pallas_call(
        totals_body,
        grid=(rows // tile,),
        in_specs=[pl.BlockSpec((tile, width), lambda g: (g, 0))],
        out_specs=[
            pl.BlockSpec((tile // NB, 1, NB), lambda g: (g, 0, 0)),
            pl.BlockSpec((tile, width), lambda g: (g, 0)),
        ],
        out_shape=[
            jax.ShapeDtypeStruct((rows // NB, 1, NB), F32),
            jax.ShapeDtypeStruct((rows, width), jnp.int8),
        ],
        name="row_sums",
        cost_estimate=cost(2000 * rows * width, 1),
        compiler_params=limit(50),
    )(counts)


def weigh_body(order, small, base, log_ctx, omega, *refs):
    w, send, keep = refs[-3:]
    tile, width = w.shape
    step = min(2048, width)
    column = jnp.concatenate(
        [jnp.sum(jnp.where(eye(NB), base[i], 0.0), axis=1, keepdims=True) for i in range(tile // NB)]
    )
    acc = jnp.zeros((tile, omega.shape[1]), F32)
    for c in range(0, width, step):
        here = slice(c, c + step)
        for r in range(0, tile, 32):
            rows = slice(r, r + 32)
            count = small[rows, here].astype(F32) + 128.0
            value = jnp.log(count) + (column[rows] - log_ctx[:, here])
            w[rows, here] = jnp.maximum(value, 0.0).astype(BF16)
        acc = acc + jnp.dot(w[:, here], omega[here, :], preferred_element_type=F32)

    @pl.when(pl.program_id(0) < 2)
    def _():
        send[0] = acc.astype(BF16)

    @pl.when(pl.program_id(0) >= 2)
    def _():
        keep[0] = acc


def weigh(small, base, log_ctx, omega, w, order, offset, tile, tokens):
    n = order.shape[0]
    rows, width = small.shape
    size = omega.shape[1]
    share = rows // n
    place = lambda g, o: (o[g] * (share // tile) + offset // tile, 0)
    held = ([] if w is None else [w]) + tokens
    return pl.pallas_call(
        weigh_body,
        grid_spec=pltpu.PrefetchScalarGridSpec(
            num_scalar_prefetch=1,
            grid=(n,),
            in_specs=[
                pl.BlockSpec((tile, width), place),
                pl.BlockSpec((tile // NB, 1, NB), lambda g, o: place(g, o) + (0,)),
                pl.BlockSpec((1, width), lambda g, o: (0, 0)),
                VMEM,
            ]
            + [ANY] * len(held),
            out_specs=[
                pl.BlockSpec((tile, width), place),
                pl.BlockSpec((1, tile, size), lambda g, o: (jnp.minimum(g, 1), 0, 0)),
                pl.BlockSpec((1, tile, size), lambda g, o: (jnp.maximum(g - 2, 0), 0, 0)),
            ],
        ),
        out_shape=[
            jax.ShapeDtypeStruct((rows, width), BF16),
            jax.ShapeDtypeStruct((2, tile, size), BF16),
            jax.ShapeDtypeStruct((2, tile, size), F32),
        ],
        input_output_aliases={} if w is None else {5: 0},
        name="weigh_and_sketch",
        cost_estimate=cost(40 * n * tile * width * size, 6 * n * tile * width),
        compiler_params=limit(44),
    )(order, small, base, log_ctx, omega, *held)


PACKED = (((0, 0), (0, 1), (0, 2), (0, 3), (3, 3)), ((1, 1), (1, 2), (1, 3), (2, 2), (2, 3)))


def gram_body(parts_of, *refs):
    n = sum(len(parts) for parts in parts_of)
    terms, (sketch, sketch_b, packed), held, arrival = refs[:n], refs[n : n + 3], refs[n + 3 : -1], refs[-1]
    which = [at for parts in parts_of for at in parts]
    copies = [
        pltpu.make_async_copy(terms[i] if at is None else terms[i].at[at], held[i], arrival.at[i])
        for i, at in enumerate(which)
    ]
    for copy in copies:
        copy.start()
    at, i = 0, 0
    for parts in parts_of:
        total = None
        for _ in parts:
            copies[i].wait()
            value = held[i][...].astype(F32)
            total = value if total is None else total + value
            i += 1
        sketch[at : at + total.shape[0], :] = total
        at += total.shape[0]
    sketch_b[...] = sketch[...].astype(BF16)
    size = sketch.shape[1] // 4
    col = lambda i, j: sketch[:, i * size : j * size]
    for i, j, half, at in ((0, 4, 0, 0), (3, 4, 0, 4), (1, 4, 1, 0), (2, 4, 1, 3)):
        packed[half * size : (half + 1) * size, at * size : (at + j - i) * size] = dot(
            col(i, i + 1), col(i, j), ROWS, HIGHEST
        )


def gram_of(pieces):
    terms = [array for piece in pieces for array, _ in piece]
    parts_of = [[which for _, which in piece] for piece in pieces]
    size = terms[0].shape[-1]
    rows = sum(piece[0][0].shape[-2] for piece in pieces)
    return pl.pallas_call(
        functools.partial(gram_body, parts_of),
        grid=(1,),
        in_specs=[HBM] * len(terms),
        out_specs=[whole(rows, size), whole(rows, size), whole(size // 2, size // 4 * 5)],
        out_shape=[
            jax.ShapeDtypeStruct((rows, size), F32),
            jax.ShapeDtypeStruct((rows, size), BF16),
            jax.ShapeDtypeStruct((size // 2, size // 4 * 5), F32),
        ],
        scratch_shapes=[pltpu.VMEM(x.shape[-2:], x.dtype) for x in terms]
        + [pltpu.SemaphoreType.DMA((len(terms),))],
        name="gram",
        cost_estimate=cost(12 * rows * size * size, 8 * rows * size),
        compiler_params=limit(32),
    )(*terms)


def eliminate(tiles):
    shape = tiles[0].shape
    lane = lax.broadcasted_iota(jnp.int32, shape, 1)
    sub = lax.broadcasted_iota(jnp.int32, shape, 0)
    spread = lambda x: jnp.broadcast_to(x, shape)
    tiles = list(tiles)
    for j in range(0, NB, 2):
        t, s = divmod(j, 8)
        first = {i: spread(tiles[i][:, j : j + 1]) for i in range(t, len(tiles))}
        second = {i: spread(tiles[i][:, j + 1 : j + 2]) for i in range(t, len(tiles))}
        a = spread(first[t][s : s + 1])
        b = spread(first[t][s + 1 : s + 2])
        c = spread(second[t][s + 1 : s + 2])
        at_first, at_second = lane == j, lane == j + 1
        pair = at_first | at_second
        row_a = jnp.where(pair, jnp.where(at_first, 1.0, 0.0), spread(tiles[t][s : s + 1]))
        row_b = jnp.where(pair, jnp.where(at_second, 1.0, 0.0), spread(tiles[t][s + 1 : s + 2]))
        over = 1.0 / (a * c - b * b)
        use_a = (c * row_a - b * row_b) * over
        use_b = (a * row_b - b * row_a) * over
        done_a = row_a * lax.rsqrt(a)
        done_b = use_b * lax.rsqrt(a * over)
        for i in range(t, len(tiles)):
            new = jnp.where(pair, 0.0, tiles[i]) - first[i] * use_a - second[i] * use_b
            if i == t:
                kept = jnp.where(sub == s, done_a, jnp.where(sub == s + 1, done_b, tiles[i]))
                new = jnp.where(sub > s + 1, new, kept)
            tiles[i] = new
    return tiles


def factor_body(core, mine, other, out, halves, t):
    size = t.shape[0]
    n = size // NB
    block = lambda i: slice(i * NB, (i + 1) * NB)
    halves[core[0]] = mine[...]
    halves[1 - core[0]] = other[...]
    trace = jnp.float32(0.0)
    for half in range(2):
        for at, (i, j) in enumerate(PACKED[half]):
            value = halves[half, :, block(at)]
            t[block(i), block(j)] = value
            if i == j:
                trace = trace + jnp.sum(jnp.where(eye(NB), value, 0.0))
    amount = jnp.float32(0.0001) * trace / jnp.float32(size)
    lower = lax.broadcasted_iota(jnp.int32, (NB, NB), 1) <= lax.broadcasted_iota(jnp.int32, (NB, NB), 0)
    for p in range(n):
        here, before = block(p), slice(0, p * NB)
        diagonal = t[here, here] + jnp.where(eye(NB), amount, 0.0)
        tiles = eliminate([diagonal[8 * i : 8 * i + 8] for i in range(NB // 8)])
        inverse = jnp.where(lower, jnp.concatenate(tiles, 0), 0.0)
        out[here, here] = inverse
        if p:
            left = dot(inverse, t[here, before], ((1,), (0,)), HIGHEST)
            out[here, before] = left
        if p < n - 1:
            rest = slice((p + 1) * NB, size)
            out[here, rest] = jnp.zeros((NB, size - (p + 1) * NB), F32)
            right = dot(inverse, t[here, rest], ((1,), (0,)), HIGHEST)
            for q in range(p + 1, n):
                off = (q - p - 1) * NB
                use = right[:, off : off + NB]
                t[block(q), q * NB :] = t[block(q), q * NB :] - dot(use, right[:, off:], ROWS, HIGHEST)
                t[block(q), here] = -dot(use, inverse, ROWS, HIGHEST)
                if p:
                    t[block(q), before] = t[block(q), before] - dot(use, left, ROWS, HIGHEST)


def factor_inverse(core, mine, other):
    size = mine.shape[0] * 4
    return pl.pallas_call(
        factor_body,
        grid=(1,),
        in_specs=[SMEM, whole(*mine.shape), whole(*mine.shape)],
        out_specs=whole(size, size),
        out_shape=jax.ShapeDtypeStruct((size, size), F32),
        scratch_shapes=[pltpu.VMEM((2,) + mine.shape, F32), pltpu.VMEM((size, size), F32)],
        name="factor_inverse",
        cost_estimate=cost(2 * size**3 * 40, 8 * size * size),
        compiler_params=limit(32),
    )(core, mine, other)


def basis_body(inverse, sketch, *refs):
    refs[-1][...] = dot(sketch[...], inverse[...], COLS, HIGHEST)


def basis_of(inverse, sketch, tokens):
    rows, size = sketch.shape
    return pl.pallas_call(
        basis_body,
        grid=(1,),
        in_specs=[whole(size, size), whole(rows, size)] + [ANY] * len(tokens),
        out_specs=whole(rows, size),
        out_shape=jax.ShapeDtypeStruct((rows, size), F32),
        name="basis",
        cost_estimate=cost(1, 1),
        compiler_params=limit(48),
    )(inverse, sketch, *tokens)


def turned_body(place, inverse, *refs):
    shares, turned = refs[:-1], refs[-1]
    rows, size = shares[0].shape
    quarter = size // 4
    for i in range(4):
        take = inverse[pl.ds(pl.multiple_of(place[i] * quarter, quarter), quarter), :]
        high = take.astype(BF16)
        low = (take - high.astype(F32)).astype(BF16)
        for d, share in enumerate(shares):
            value = dot(high, share[...], COLS) + dot(low, share[...], COLS)
            start = pl.multiple_of(place[4 + d] * rows, rows)
            turned[i * quarter : (i + 1) * quarter, pl.ds(start, rows)] = value.astype(BF16)


def turned_basis(place, inverse, shares):
    rows, size = shares[0].shape
    n = len(shares)
    return pl.pallas_call(
        turned_body,
        grid=(1,),
        in_specs=[SMEM, whole(size, size)] + [whole(rows, size)] * n,
        out_specs=whole(size, n * rows),
        out_shape=jax.ShapeDtypeStruct((size, n * rows), BF16),
        name="turned_basis",
        cost_estimate=cost(4 * n * rows * size * size, 4 * n * rows * size),
        compiler_params=limit(48),
    )(place, inverse, *shares)


def project_body(turned, w, *refs):
    send, own = refs[-2:]
    half = send.shape[0]
    value = jnp.dot(turned[...], w[...], preferred_element_type=F32)
    send[...] = value[:half].astype(BF16)
    own[...] = value[half:]


def project(turned, w, tokens, start, width, tile):
    size, rows = turned.shape
    steps = width // tile
    first = start // tile
    out = lambda g: (0, g)
    return pl.pallas_call(
        project_body,
        grid=(steps,),
        in_specs=[
            VMEM,
            pl.BlockSpec((rows, tile), lambda g: (0, first + g)),
        ]
        + [ANY] * len(tokens),
        out_specs=[pl.BlockSpec((size // 2, tile), out), pl.BlockSpec((size // 2, tile), out)],
        out_shape=[
            jax.ShapeDtypeStruct((size // 2, width), BF16),
            jax.ShapeDtypeStruct((size // 2, width), F32),
        ],
        name="project",
        cost_estimate=cost(40 * rows * size * width, 2 * rows * width),
        compiler_params=limit(48),
    )(turned, w, *tokens)


def finish_body(scale, mine, core_term, chip_term, *refs):
    total = mine[...] + core_term[...].astype(F32) + chip_term[...].astype(F32)
    refs[-1][...] = jnp.transpose(total * scale)


def finish(own, core_term, chip_term, out, start, full, tile, scale):
    size, width = chip_term.shape
    first = start // tile
    held = [] if out is None else [out]
    return pl.pallas_call(
        functools.partial(finish_body, scale),
        grid=(width // tile,),
        in_specs=[
            pl.BlockSpec((size, tile), lambda g: (1, g)),
            pl.BlockSpec((size, tile), lambda g: (1, g)),
            pl.BlockSpec((size, tile), lambda g: (0, g)),
        ]
        + [ANY] * len(held),
        out_specs=pl.BlockSpec((tile, size), lambda g: (first + g, 0)),
        out_shape=jax.ShapeDtypeStruct((full, size), F32),
        input_output_aliases={3: 0} if held else {},
        name="finish",
        cost_estimate=cost(1, 1),
        compiler_params=limit(32),
    )(own, core_term, chip_term, *held)


def rotate(x, n, by):
    return lax.ppermute(x, "col", [(i, (i + by) % n) for i in range(n)])


def swap_col(x, bit):
    return lax.ppermute(x, "col", [(i, i ^ bit) for i in range(4)])


def swap(x, bit):
    return lax.ppermute(x, "row", [(i, i ^ bit) for i in range(4)])


def half_of(x, which):
    rows = x.shape[0] // 2
    return lax.dynamic_slice_in_dim(x, which * rows, rows, 0)


def stack_by(which, mine, other):
    return jnp.where(which == 0, jnp.concatenate([mine, other]), jnp.concatenate([other, mine]))


def pieces_of(share):
    n = share // NB
    return [2 * NB] * ((n - 2) // 2) + [NB] * (n - (n - 2) // 2 * 2) if n > 2 else [NB] * n


def sketch_phase(counts, log_ctx, ctx_sum, omega, col):
    rows, width = counts.shape
    part, small = row_sums(counts)
    part = jnp.concatenate([part.reshape(rows // NB, NB), jnp.broadcast_to(ctx_sum, (8, NB))])
    part = part + swap_col(part, 1)
    part = part + swap_col(part, 2)
    logs = jnp.log(part)
    base = logs[-1, 0] - jnp.log(F32(5.0)) - logs[:-8]
    base = base.reshape(rows // NB, 1, NB)
    order = jnp.stack([col ^ 1, col ^ 3, col ^ 2, col])
    w, offset, pieces, passed, arrived = None, 0, [], [], []
    for k, tile in enumerate(pieces_of(rows // 4)):
        tokens = passed[k - 2 : k - 1] if k >= 2 else []
        tokens = tokens + (arrived[k - 3 : k - 2] if k >= 3 else [])
        w, send, keep = weigh(small, base, log_ctx, omega, w, order, offset, tile, tokens)
        offset += tile
        near = swap_col(send, 1)
        passed.append((keep[0] + near[1].astype(F32)).astype(BF16))
        arrived.append(swap_col(passed[k], 2))
        pieces.append([(keep, 1), (near, 0), (arrived[k], None)])
    return w, pieces


def sketch_phase_any(counts, log_ctx, ctx_sum, omega, col):
    row_part = jnp.sum(counts.astype(F32), axis=1)
    row_total, ctx_total = lax.psum((row_part, ctx_sum), "col")
    value = jnp.log(counts.astype(F32)) + (
        jnp.log(ctx_total) - jnp.log(F32(5.0)) - jnp.log(row_total)[:, None] - log_ctx
    )
    w = jnp.maximum(value, 0.0).astype(BF16)
    partial = jnp.dot(w, omega, preferred_element_type=F32)
    return w, [[(lax.psum_scatter(partial, "col", scatter_dimension=0, tiled=True), None)]]


def shards(counts, ctx_counts, omega):
    rows, width = counts.shape
    n = lax.axis_size("col")
    row = lax.axis_index("row")
    col = lax.axis_index("col")
    core, chip = row % 2, row // 2
    ctx_weight = ctx_counts.astype(F32) ** 0.75
    ctx_sum = jnp.sum(ctx_weight)
    log_ctx = jnp.log(ctx_weight)[None, :]
    direct = n == 4 and rows % (4 * NB) == 0
    phase = sketch_phase if direct else sketch_phase_any
    w, pieces = phase(counts, log_ctx, ctx_sum, omega, col)
    sketch, sketch_b, packed = gram_of(pieces)
    half = half_of(packed, core) + swap(half_of(packed, 1 - core), 1)
    quarter = half_of(half, chip) + swap(half_of(half, 1 - chip), 2)
    if direct:
        quarter = quarter + swap_col(quarter, 1)
        quarter = quarter + swap_col(quarter, 2)
        shares = [sketch_b] + [rotate(sketch_b, n, d) for d in range(1, n)]
        sources = [(col - d) % n for d in range(n)]
    else:
        quarter = lax.psum(quarter, "col")
        shares = [lax.all_gather(sketch_b, "col", tiled=True)]
        sources = [jnp.int32(0)]
    half = stack_by(chip, quarter, swap(quarter, 2))
    inverse = factor_inverse(core.reshape(1), half, swap(half, 1))
    place = jnp.stack([row ^ 3, row ^ 1, row ^ 2, row] + sources)
    turned = turned_basis(place, inverse, shares)
    eighth = width // 8
    tile = min(512, eighth)
    scale = float(1.0 / (rows * lax.axis_size("row")) ** 0.5)
    quarter = omega.shape[1] // 4
    out, start = None, 0
    sent, passed, arrived = [], [], []
    for j, pieces in enumerate((1, 1, 2, 2, 1, 1)):
        piece = pieces * eighth
        tokens = sent[-1:] + (passed[-2:-1] if j >= 2 else []) + (arrived[-3:-2] if j >= 3 else [])
        send, mine = project(turned, w, tokens, start, piece, tile)
        core_term = swap(send, 1)
        chip_send = (mine[:quarter] + core_term[:quarter].astype(F32)).astype(BF16)
        chip_term = swap(chip_send, 2)
        sent.append(send)
        passed.append(chip_send)
        arrived.append(chip_term)
        out = finish(mine, core_term, chip_term, out, start, width, eighth, scale)
        start += piece
    basis = basis_of(inverse, sketch, sent[-1:])
    return (basis, out)


def solution(mesh):
    in_specs = (P(("grp", "row"), "col"), P(("grp", "col")), P("col", None))
    out_specs = (P(("grp", "row", "col"), None), P(("grp", "col"), "row"))
    return jax.shard_map(shards, mesh=mesh, in_specs=in_specs, out_specs=out_specs, check_vma=False)
```

```python
import functools

import jax
import jax.numpy as jnp
from jax import lax
from jax.experimental import pallas as pl
from jax.experimental.pallas import tpu as pltpu
from jax.sharding import PartitionSpec as P

HIGHEST = lax.Precision.HIGHEST
F32 = jnp.float32
BF16 = jnp.bfloat16
NB = 128
ROWS = ((0,), (0,))
COLS = ((1,), (1,))
VMEM = pl.BlockSpec(memory_space=pltpu.VMEM)
SMEM = pl.BlockSpec(memory_space=pltpu.SMEM)
ANY = pl.BlockSpec(memory_space=pl.ANY)
HBM = pl.BlockSpec(memory_space=pltpu.HBM)


def limit(mib):
    return pltpu.CompilerParams(vmem_limit_bytes=mib * 1024 * 1024)


def cost(flops, nbytes):
    return pl.CostEstimate(flops=int(flops), bytes_accessed=int(nbytes), transcendentals=0)


def whole(*shape):
    return pl.BlockSpec(shape, lambda *_: (0,) * len(shape))


def dot(a, b, contract, precision=None):
    return lax.dot_general(a, b, (contract, ((), ())), precision=precision, preferred_element_type=F32)


def eye(n):
    return lax.broadcasted_iota(jnp.int32, (n, n), 0) == lax.broadcasted_iota(jnp.int32, (n, n), 1)


def totals_body(counts, out, small):
    tile, width = counts.shape
    for at in range(tile // NB):
        parts = []
        for r in range(at * NB, (at + 1) * NB, 32):
            acc = None
            for c in range(0, width, NB):
                value = counts[r : r + 32, c : c + NB]
                small[r : r + 32, c : c + NB] = (value - 128).astype(jnp.int8)
                acc = value if acc is None else acc + value
            parts.append(jnp.sum(acc.astype(F32), axis=1, keepdims=True))
        column = jnp.concatenate(parts, 0)
        out[at] = jnp.sum(jnp.where(eye(NB), column, 0.0), axis=0, keepdims=True)


def row_sums(counts):
    rows, width = counts.shape
    tile = 2 * NB
    return pl.pallas_call(
        totals_body,
        grid=(rows // tile,),
        in_specs=[pl.BlockSpec((tile, width), lambda g: (g, 0))],
        out_specs=[
            pl.BlockSpec((tile // NB, 1, NB), lambda g: (g, 0, 0)),
            pl.BlockSpec((tile, width), lambda g: (g, 0)),
        ],
        out_shape=[
            jax.ShapeDtypeStruct((rows // NB, 1, NB), F32),
            jax.ShapeDtypeStruct((rows, width), jnp.int8),
        ],
        name="row_sums",
        cost_estimate=cost(2000 * rows * width, 1),
        compiler_params=limit(50),
    )(counts)


def weigh_body(order, small, base, log_ctx, omega, *refs):
    w, send, keep = refs[-3:]
    tile, width = w.shape
    step = min(2048, width)
    column = jnp.concatenate(
        [jnp.sum(jnp.where(eye(NB), base[i], 0.0), axis=1, keepdims=True) for i in range(tile // NB)]
    )
    acc = jnp.zeros((tile, omega.shape[1]), F32)
    for c in range(0, width, step):
        here = slice(c, c + step)
        for r in range(0, tile, 32):
            rows = slice(r, r + 32)
            count = small[rows, here].astype(F32) + 128.0
            value = jnp.log(count) + (column[rows] - log_ctx[:, here])
            w[rows, here] = jnp.maximum(value, 0.0).astype(BF16)
        acc = acc + jnp.dot(w[:, here], omega[here, :], preferred_element_type=F32)

    @pl.when(pl.program_id(0) < 2)
    def _():
        send[0] = acc.astype(BF16)

    @pl.when(pl.program_id(0) >= 2)
    def _():
        keep[0] = acc


def weigh(small, base, log_ctx, omega, w, order, offset, tile, tokens):
    n = order.shape[0]
    rows, width = small.shape
    size = omega.shape[1]
    share = rows // n
    place = lambda g, o: (o[g] * (share // tile) + offset // tile, 0)
    held = ([] if w is None else [w]) + tokens
    return pl.pallas_call(
        weigh_body,
        grid_spec=pltpu.PrefetchScalarGridSpec(
            num_scalar_prefetch=1,
            grid=(n,),
            in_specs=[
                pl.BlockSpec((tile, width), place),
                pl.BlockSpec((tile // NB, 1, NB), lambda g, o: place(g, o) + (0,)),
                pl.BlockSpec((1, width), lambda g, o: (0, 0)),
                VMEM,
            ]
            + [ANY] * len(held),
            out_specs=[
                pl.BlockSpec((tile, width), place),
                pl.BlockSpec((1, tile, size), lambda g, o: (jnp.minimum(g, 1), 0, 0)),
                pl.BlockSpec((1, tile, size), lambda g, o: (jnp.maximum(g - 2, 0), 0, 0)),
            ],
        ),
        out_shape=[
            jax.ShapeDtypeStruct((rows, width), BF16),
            jax.ShapeDtypeStruct((2, tile, size), BF16),
            jax.ShapeDtypeStruct((2, tile, size), F32),
        ],
        input_output_aliases={} if w is None else {5: 0},
        name="weigh_and_sketch",
        cost_estimate=cost(40 * n * tile * width * size, 6 * n * tile * width),
        compiler_params=limit(44),
    )(order, small, base, log_ctx, omega, *held)


PACKED = (((0, 0), (0, 1), (0, 2), (0, 3), (3, 3)), ((1, 1), (1, 2), (1, 3), (2, 2), (2, 3)))


def gram_body(parts_of, core, *refs):
    n = sum(len(parts) for parts in parts_of)
    terms, (sketch, sketch_b, own, send) = refs[:n], refs[n : n + 4]
    held, arrival = refs[n + 4 : -1], refs[-1]
    which = [at for parts in parts_of for at in parts]
    copies = [
        pltpu.make_async_copy(terms[i] if at is None else terms[i].at[at], held[i], arrival.at[i])
        for i, at in enumerate(which)
    ]
    for copy in copies:
        copy.start()
    at, i = 0, 0
    for parts in parts_of:
        total = None
        for _ in parts:
            copies[i].wait()
            value = held[i][...].astype(F32)
            total = value if total is None else total + value
            i += 1
        sketch[at : at + total.shape[0], :] = total
        at += total.shape[0]
    sketch_b[...] = sketch[...].astype(BF16)
    size = sketch.shape[1] // 4
    col = lambda i, j: sketch[:, i * size : j * size]
    upper = lambda i, j: dot(col(i, i + 1), col(i, j), ROWS, HIGHEST)
    halves = [
        jnp.concatenate([upper(0, 4), upper(3, 4)], axis=1),
        jnp.concatenate([upper(1, 4), upper(2, 4)], axis=1),
    ]
    for which in range(2):

        @pl.when(core[0] == which)
        def _(which=which):
            own[...] = halves[which]
            send[...] = halves[1 - which]


def gram_of(core, pieces):
    terms = [array for piece in pieces for array, _ in piece]
    parts_of = [[which for _, which in piece] for piece in pieces]
    size = terms[0].shape[-1]
    rows = sum(piece[0][0].shape[-2] for piece in pieces)
    return pl.pallas_call(
        functools.partial(gram_body, parts_of),
        grid=(1,),
        in_specs=[SMEM] + [HBM] * len(terms),
        out_specs=[whole(rows, size)] * 2 + [whole(size // 4, size // 4 * 5)] * 2,
        out_shape=[
            jax.ShapeDtypeStruct((rows, size), F32),
            jax.ShapeDtypeStruct((rows, size), BF16),
            jax.ShapeDtypeStruct((size // 4, size // 4 * 5), F32),
            jax.ShapeDtypeStruct((size // 4, size // 4 * 5), F32),
        ],
        scratch_shapes=[pltpu.VMEM(x.shape[-2:], x.dtype) for x in terms]
        + [pltpu.SemaphoreType.DMA((len(terms),))],
        name="gram",
        cost_estimate=cost(12 * rows * size * size, 8 * rows * size),
        compiler_params=limit(60),
    )(core, *terms)


def small_inverse(g):
    n = len(g)
    g = [list(r) for r in g]
    m = [[None] * n for _ in range(n)]
    out = [[None] * n for _ in range(n)]
    for j in range(0, n, 2):
        k = j + 1
        a, b, c = g[j][j], g[k][j], g[k][k]
        over = 1.0 / (a * c - b * b)
        ca, cb, cc = a * over, b * over, c * over
        ra, rb = lax.rsqrt(a), lax.rsqrt(ca)
        for l in range(j):
            out[j][l] = m[j][l] * ra
            out[k][l] = (ca * m[k][l] - cb * m[j][l]) * rb
        out[j][j], out[k][j], out[k][k] = ra, -cb * rb, ca * rb
        for i in range(k + 1, n):
            f = cc * g[i][j] - cb * g[i][k]
            h = ca * g[i][k] - cb * g[i][j]
            for l in range(k + 1, i + 1):
                g[i][l] = g[i][l] - (f * g[l][j] + h * g[l][k])
            for l in range(j):
                m[i][l] = m[i][l] - (f * m[j][l] + h * m[k][l])
            m[i][j], m[i][k] = -f, -h
    return out


def total(terms):
    while len(terms) > 1:
        terms = [x + y for x, y in zip(terms[::2], terms[1::2])] + terms[len(terms) // 2 * 2 :]
    return terms[0]


def eliminate(tiles, done):
    shape, n, group = tiles[0].shape, len(tiles), 2
    lane = lax.broadcasted_iota(jnp.int32, shape, 1)
    sub = lax.broadcasted_iota(jnp.int32, shape, 0)
    spread = lambda x: jnp.broadcast_to(x, shape)
    columns = lambda x: tuple(spread(x[:, m : m + 1]) for m in range(8))
    pivots = lane < 8

    def turn(t, carry):
        here, tiles = carry
        g = [[spread(here[l][i : i + 1]) for l in range(i + 1)] for i in range(8)]
        rows = [
            jnp.where(pivots, jnp.where(lane == k, 1.0, 0.0), spread(tiles[0][k : k + 1])) for k in range(8)
        ]
        low = small_inverse(g)
        y = [total([low[r][k] * rows[k] for k in range(r + 1)]) for r in range(8)]
        z = [total([low[r][m] * y[r] for r in range(m, 8)]) for m in range(8)]
        new = []
        for x in tiles[1:]:
            x = jnp.where(pivots, 0.0, x) - total([c * w for c, w in zip(columns(x), z)])
            new.append(pltpu.roll(x, NB - 8, 1))
            if len(new) == 1:
                here = columns(new[0])
        final = y[0]
        for r in range(1, 8):
            final = jnp.where(sub == r, y[r], final)
        done[pl.ds(pl.multiple_of(8 * t, 8), 8), :] = final
        return here, tuple(new) + (jnp.zeros(shape, F32),)

    carry = columns(tiles[0]), tuple(tiles)
    for start in range(0, n, group):
        here, tiles = lax.fori_loop(start, start + group, turn, carry)
        carry = here, tiles[: n - start - group]
    return [done[0:8, :]] + [pltpu.roll(done[8 * t : 8 * t + 8, :], 8 * t, 1) for t in range(1, n)]


def factor_body(core, mine, other, out, halves, t, done):
    size = t.shape[0]
    n = size // NB
    block = lambda i: slice(i * NB, (i + 1) * NB)
    halves[core[0]] = mine[...]
    halves[1 - core[0]] = other[...]
    trace = jnp.float32(0.0)
    for half in range(2):
        for at, (i, j) in enumerate(PACKED[half]):
            value = halves[half, :, block(at)]
            t[block(i), block(j)] = value
            if i == j:
                trace = trace + jnp.sum(jnp.where(eye(NB), value, 0.0))
    amount = jnp.float32(0.0001) * trace / jnp.float32(size)
    lower = lax.broadcasted_iota(jnp.int32, (NB, NB), 1) <= lax.broadcasted_iota(jnp.int32, (NB, NB), 0)
    for p in range(n):
        here, before = block(p), slice(0, p * NB)
        diagonal = t[here, here] + jnp.where(eye(NB), amount, 0.0)
        tiles = eliminate([diagonal[8 * i : 8 * i + 8] for i in range(NB // 8)], done)
        inverse = jnp.where(lower, jnp.concatenate(tiles, 0), 0.0)
        out[here, here] = inverse
        if p:
            left = dot(inverse, t[here, before], ((1,), (0,)), HIGHEST)
            out[here, before] = left
        if p < n - 1:
            rest = slice((p + 1) * NB, size)
            out[here, rest] = jnp.zeros((NB, size - (p + 1) * NB), F32)
            right = dot(inverse, t[here, rest], ((1,), (0,)), HIGHEST)
            for q in range(p + 1, n):
                off = (q - p - 1) * NB
                use = right[:, off : off + NB]
                t[block(q), q * NB :] = t[block(q), q * NB :] - dot(use, right[:, off:], ROWS, HIGHEST)
                t[block(q), here] = -dot(use, inverse, ROWS, HIGHEST)
                if p:
                    t[block(q), before] = t[block(q), before] - dot(use, left, ROWS, HIGHEST)


def factor_inverse(core, mine, other):
    size = mine.shape[0] * 4
    return pl.pallas_call(
        factor_body,
        grid=(1,),
        in_specs=[SMEM, whole(*mine.shape), whole(*mine.shape)],
        out_specs=whole(size, size),
        out_shape=jax.ShapeDtypeStruct((size, size), F32),
        scratch_shapes=[
            pltpu.VMEM((2,) + mine.shape, F32),
            pltpu.VMEM((size, size), F32),
            pltpu.VMEM((NB, NB), F32),
        ],
        name="factor_inverse",
        cost_estimate=cost(1, 1),
        compiler_params=limit(24),
    )(core, mine, other)


def basis_body(inverse, sketch, *refs):
    refs[-1][...] = dot(sketch[...], inverse[...], COLS, HIGHEST)


def basis_of(inverse, sketch, tokens):
    rows, size = sketch.shape
    return pl.pallas_call(
        basis_body,
        grid=(1,),
        in_specs=[whole(size, size), whole(rows, size)] + [ANY] * len(tokens),
        out_specs=whole(rows, size),
        out_shape=jax.ShapeDtypeStruct((rows, size), F32),
        name="basis",
        cost_estimate=cost(1, 1),
        compiler_params=limit(24),
    )(inverse, sketch, *tokens)


def turned_body(place, inverse, *refs):
    shares, turned = refs[:-1], refs[-1]
    rows, size = shares[0].shape
    quarter = size // 4
    for i in range(4):
        take = inverse[pl.ds(pl.multiple_of(place[i] * quarter, quarter), quarter), :]
        high = take.astype(BF16)
        low = (take - high.astype(F32)).astype(BF16)
        for d, share in enumerate(shares):
            value = dot(high, share[...], COLS) + dot(low, share[...], COLS)
            start = pl.multiple_of(place[4 + d] * rows, rows)
            turned[i * quarter : (i + 1) * quarter, pl.ds(start, rows)] = value.astype(BF16)


def turned_basis(place, inverse, shares):
    rows, size = shares[0].shape
    n = len(shares)
    return pl.pallas_call(
        turned_body,
        grid=(1,),
        in_specs=[SMEM, whole(size, size)] + [whole(rows, size)] * n,
        out_specs=whole(size, n * rows),
        out_shape=jax.ShapeDtypeStruct((size, n * rows), BF16),
        name="turned_basis",
        cost_estimate=cost(4 * n * rows * size * size, 4 * n * rows * size),
        compiler_params=limit(24),
    )(place, inverse, *shares)


def project_body(turned, w, *refs):
    send, own = refs[-2:]
    half = send.shape[0]
    value = jnp.dot(turned[...], w[...], preferred_element_type=F32)
    send[...] = value[:half].astype(BF16)
    own[...] = value[half:]


def project(turned, w, tokens, start, width, tile):
    size, rows = turned.shape
    steps = width // tile
    first = start // tile
    out = lambda g: (0, g)
    return pl.pallas_call(
        project_body,
        grid=(steps,),
        in_specs=[
            pl.BlockSpec((size, rows), lambda g: (0, 0), pipeline_mode=pl.Buffered(1)),
            pl.BlockSpec((rows, tile), lambda g: (0, first + g)),
        ]
        + [ANY] * len(tokens),
        out_specs=[pl.BlockSpec((size // 2, tile), out), pl.BlockSpec((size // 2, tile), out)],
        out_shape=[
            jax.ShapeDtypeStruct((size // 2, width), BF16),
            jax.ShapeDtypeStruct((size // 2, width), F32),
        ],
        name="project",
        cost_estimate=cost(40 * rows * size * width, 2 * rows * width),
        compiler_params=limit(40),
    )(turned, w, *tokens)


def finish_body(scale, start, mine, core_term, chip_term, *refs):
    out, turned, arrival = refs[-3:]
    total = mine[...] + core_term[...].astype(F32) + chip_term[...].astype(F32)
    turned[...] = jnp.transpose(total * scale)
    copy = pltpu.make_async_copy(turned, out.at[pl.ds(start, turned.shape[0])], arrival)
    copy.start()
    copy.wait()


def finish(own, core_term, chip_term, out, start, full, scale):
    size, width = chip_term.shape
    held = [] if out is None else [out]
    return pl.pallas_call(
        functools.partial(finish_body, scale, start),
        grid=(1,),
        in_specs=[
            pl.BlockSpec((size, width), lambda g: (1, 0)),
            pl.BlockSpec((size, width), lambda g: (1, 0)),
            whole(size, width),
        ]
        + [ANY] * len(held),
        out_specs=ANY,
        out_shape=jax.ShapeDtypeStruct((full, size), F32),
        input_output_aliases={3: 0} if held else {},
        scratch_shapes=[pltpu.VMEM((width, size), F32), pltpu.SemaphoreType.DMA],
        name="finish",
        cost_estimate=cost(1, 1),
        compiler_params=limit(24),
    )(own, core_term, chip_term, *held)


def pass_body(mine, core_term, *refs):
    refs[-1][...] = (mine[...] + core_term[...].astype(F32)).astype(BF16)


def pass_on(own, core_term, tokens):
    size, width = own.shape[0] // 2, own.shape[1]
    return pl.pallas_call(
        pass_body,
        grid=(1,),
        in_specs=[whole(size, width), whole(size, width)] + [ANY] * len(tokens),
        out_specs=whole(size, width),
        out_shape=jax.ShapeDtypeStruct((size, width), BF16),
        name="pass_on",
        cost_estimate=cost(1, 1),
        compiler_params=limit(24),
    )(own, core_term, *tokens)


def rotate(x, n, by):
    return lax.ppermute(x, "col", [(i, (i + by) % n) for i in range(n)])


def swap_col(x, bit):
    return lax.ppermute(x, "col", [(i, i ^ bit) for i in range(4)])


def swap(x, bit):
    return lax.ppermute(x, "row", [(i, i ^ bit) for i in range(4)])


def half_of(x, which):
    rows = x.shape[0] // 2
    return lax.dynamic_slice_in_dim(x, which * rows, rows, 0)


def stack_by(which, mine, other):
    return jnp.where(which == 0, jnp.concatenate([mine, other]), jnp.concatenate([other, mine]))


def pieces_of(share):
    n = share // NB
    return [2 * NB] * ((n - 2) // 2) + [NB] * (n - (n - 2) // 2 * 2) if n > 2 else [NB] * n


def sketch_phase(counts, log_ctx, ctx_sum, omega, col):
    rows, width = counts.shape
    part, small = row_sums(counts)
    part = jnp.concatenate([part.reshape(rows // NB, NB), jnp.broadcast_to(ctx_sum, (8, NB))])
    part = part + swap_col(part, 1)
    part = part + swap_col(part, 2)
    logs = jnp.log(part)
    base = logs[-1, 0] - jnp.log(F32(5.0)) - logs[:-8]
    base = base.reshape(rows // NB, 1, NB)
    order = jnp.stack([col ^ 1, col ^ 3, col ^ 2, col])
    w, offset, pieces, passed, arrived = None, 0, [], [], []
    for k, tile in enumerate(pieces_of(rows // 4)):
        tokens = passed[k - 2 : k - 1] if k >= 2 else []
        tokens = tokens + (arrived[k - 3 : k - 2] if k >= 3 else [])
        w, send, keep = weigh(small, base, log_ctx, omega, w, order, offset, tile, tokens)
        offset += tile
        near = swap_col(send, 1)
        passed.append((keep[0] + near[1].astype(F32)).astype(BF16))
        arrived.append(swap_col(passed[k], 2))
        pieces.append([(keep, 1), (near, 0), (arrived[k], None)])
    return w, pieces


def sketch_phase_any(counts, log_ctx, ctx_sum, omega, col):
    row_part = jnp.sum(counts.astype(F32), axis=1)
    row_total, ctx_total = lax.psum((row_part, ctx_sum), "col")
    value = jnp.log(counts.astype(F32)) + (
        jnp.log(ctx_total) - jnp.log(F32(5.0)) - jnp.log(row_total)[:, None] - log_ctx
    )
    w = jnp.maximum(value, 0.0).astype(BF16)
    partial = jnp.dot(w, omega, preferred_element_type=F32)
    return w, [[(lax.psum_scatter(partial, "col", scatter_dimension=0, tiled=True), None)]]


def shards(counts, ctx_counts, omega):
    rows, width = counts.shape
    n = lax.axis_size("col")
    row = lax.axis_index("row")
    col = lax.axis_index("col")
    core, chip = row % 2, row // 2
    ctx_weight = ctx_counts.astype(F32) ** 0.75
    ctx_sum = jnp.sum(ctx_weight)
    log_ctx = jnp.log(ctx_weight)[None, :]
    direct = n == 4 and rows % (4 * NB) == 0
    phase = sketch_phase if direct else sketch_phase_any
    w, pieces = phase(counts, log_ctx, ctx_sum, omega, col)
    sketch, sketch_b, half, other_half = gram_of(core.reshape(1), pieces)
    half = half + swap(other_half, 1)
    quarter = half_of(half, chip) + swap(half_of(half, 1 - chip), 2)
    if direct:
        quarter = quarter + swap_col(quarter, 1)
        quarter = quarter + swap_col(quarter, 2)
        shares = [sketch_b] + [rotate(sketch_b, n, d) for d in range(1, n)]
        sources = [(col - d) % n for d in range(n)]
    else:
        quarter = lax.psum(quarter, "col")
        shares = [lax.all_gather(sketch_b, "col", tiled=True)]
        sources = [jnp.int32(0)]
    half = stack_by(chip, quarter, swap(quarter, 2))
    inverse = factor_inverse(core.reshape(1), half, swap(half, 1))
    place = jnp.stack([row ^ 3, row ^ 1, row ^ 2, row] + sources)
    turned = turned_basis(place, inverse, shares)
    widths = (1, 2, 3, 3, 4, 2, 1) if width % (16 * NB) == 0 else (1,) * 8
    unit = width // sum(widths)
    scale = float(1.0 / (rows * lax.axis_size("row")) ** 0.5)
    quarter = omega.shape[1] // 4
    out, start = None, 0
    sent, passed, arrived = [], [], []
    for j, pieces in enumerate(widths):
        piece = pieces * unit
        tokens = sent[-1:] + (passed[-2:-1] if j >= 2 else []) + (arrived[-3:-2] if j >= 3 else [])
        send, mine = project(turned, w, tokens, start, piece, unit)
        core_term = swap(send, 1)
        if j == len(widths) - 1:
            basis = basis_of(inverse, sketch, [send])
            chip_send = pass_on(mine, core_term, [arrived[-2], basis])
        else:
            chip_send = (mine[:quarter] + core_term[:quarter].astype(F32)).astype(BF16)
        chip_term = swap(chip_send, 2)
        sent.append(send)
        passed.append(chip_send)
        arrived.append(chip_term)
        out = finish(mine, core_term, chip_term, out, start, width, scale)
        start += piece
    return (basis, out)


def solution(mesh):
    in_specs = (P(("grp", "row"), "col"), P(("grp", "col")), P("col", None))
    out_specs = (P(("grp", "row", "col"), None), P(("grp", "col"), "row"))
    return jax.shard_map(shards, mesh=mesh, in_specs=in_specs, out_specs=out_specs, check_vma=False)
```

```python
import functools

import jax
import jax.numpy as jnp
from jax import lax
from jax.experimental import pallas as pl
from jax.experimental.pallas import tpu as pltpu
from jax.sharding import PartitionSpec as P

HIGHEST = lax.Precision.HIGHEST
F32 = jnp.float32
BF16 = jnp.bfloat16
NB = 128
ROWS = ((0,), (0,))
COLS = ((1,), (1,))
VMEM = pl.BlockSpec(memory_space=pltpu.VMEM)
SMEM = pl.BlockSpec(memory_space=pltpu.SMEM)
ANY = pl.BlockSpec(memory_space=pl.ANY)
HBM = pl.BlockSpec(memory_space=pltpu.HBM)


def limit(mib):
    return pltpu.CompilerParams(vmem_limit_bytes=mib * 1024 * 1024)


def cost(flops, nbytes):
    return pl.CostEstimate(flops=int(flops), bytes_accessed=int(nbytes), transcendentals=0)


def whole(*shape):
    return pl.BlockSpec(shape, lambda *_: (0,) * len(shape))


def dot(a, b, contract, precision=None):
    return lax.dot_general(a, b, (contract, ((), ())), precision=precision, preferred_element_type=F32)


def eye(n):
    return lax.broadcasted_iota(jnp.int32, (n, n), 0) == lax.broadcasted_iota(jnp.int32, (n, n), 1)


def totals_body(counts, ctx_counts, out, small):
    tile, width = counts.shape
    n = tile // NB
    step = pl.program_id(0)
    for at in range(n):
        parts = []
        for r in range(at * NB, (at + 1) * NB, 32):
            acc = None
            for c in range(0, width, NB):
                value = counts[r : r + 32, c : c + NB]
                small[r : r + 32, c : c + NB] = (value - 128).astype(jnp.int8)
                acc = value if acc is None else acc + value
            parts.append(jnp.sum(acc.astype(F32), axis=1, keepdims=True))
        column = jnp.concatenate(parts, 0)
        out[step * n + at] = jnp.sum(jnp.where(eye(NB), column, 0.0), axis=0, keepdims=True)

    @pl.when(step == 0)
    def _():
        count = ctx_counts[...].astype(F32)
        weight = jnp.sqrt(count) * jnp.sqrt(jnp.sqrt(count))
        out[out.shape[0] - 1] = jnp.broadcast_to(jnp.sum(weight, axis=1, keepdims=True), (1, NB))


def row_sums(counts, ctx_counts):
    rows, width = counts.shape
    tile = 2 * NB
    return pl.pallas_call(
        totals_body,
        grid=(rows // tile,),
        in_specs=[pl.BlockSpec((tile, width), lambda g: (g, 0)), whole(1, width)],
        out_specs=[whole(rows // NB + 1, 1, NB), pl.BlockSpec((tile, width), lambda g: (g, 0))],
        out_shape=[
            jax.ShapeDtypeStruct((rows // NB + 1, 1, NB), F32),
            jax.ShapeDtypeStruct((rows, width), jnp.int8),
        ],
        name="row_sums",
        cost_estimate=cost(2000 * rows * width, 1),
        compiler_params=limit(45),
    )(counts, ctx_counts)


def weigh_body(split, order, small, row_total, ctx_total, ctx_counts, omega, *refs):
    w, keep, *sends = refs[-4:] if split else refs[-3:]
    tile, width = w.shape
    step = min(2048, width)
    row_log = [jnp.log(ctx_total[0]) - jnp.log(F32(5.0)) - jnp.log(row_total[i]) for i in range(tile // NB)]
    column = jnp.concatenate([jnp.sum(jnp.where(eye(NB), x, 0.0), axis=1, keepdims=True) for x in row_log])
    log_ctx = 0.75 * jnp.log(ctx_counts[...].astype(F32))
    acc = jnp.zeros((tile, omega.shape[1]), F32)
    for c in range(0, width, step):
        here = slice(c, c + step)
        for r in range(0, tile, 32):
            rows = slice(r, r + 32)
            count = small[rows, here].astype(F32) + 128.0
            value = jnp.log(count) + (column[rows] - log_ctx[:, here])
            w[rows, here] = jnp.maximum(value, 0.0).astype(BF16)
        acc = acc + jnp.dot(w[:, here], omega[here, :], preferred_element_type=F32)

    if split:
        for g in range(2):

            @pl.when(pl.program_id(0) == g)
            def _(g=g):
                sends[g][...] = acc.astype(BF16)

    else:

        @pl.when(pl.program_id(0) < 2)
        def _():
            sends[0][0] = acc.astype(BF16)

    @pl.when(pl.program_id(0) >= 2)
    def _():
        keep[0] = acc


def weigh(small, totals, ctx_counts, omega, w, order, offset, tile, tokens, split):
    n = order.shape[0]
    rows, width = small.shape
    size = omega.shape[1]
    share = rows // n
    place = lambda g, o: (o[g] * (share // tile) + offset // tile, 0)
    held = ([] if w is None else [w]) + tokens
    if split:
        sends = [jax.ShapeDtypeStruct((tile, size), BF16)] * 2
        send_specs = [whole(tile, size)] * 2
    else:
        sends = [jax.ShapeDtypeStruct((2, tile, size), BF16)]
        send_specs = [pl.BlockSpec((1, tile, size), lambda g, o: (jnp.minimum(g, 1), 0, 0))]
    return pl.pallas_call(
        functools.partial(weigh_body, split),
        grid_spec=pltpu.PrefetchScalarGridSpec(
            num_scalar_prefetch=1,
            grid=(n,),
            in_specs=[
                pl.BlockSpec((tile, width), place),
                pl.BlockSpec((tile // NB, 1, NB), lambda g, o: place(g, o) + (0,)),
                pl.BlockSpec((1, 1, NB), lambda g, o: (rows // NB, 0, 0)),
                pl.BlockSpec((1, width), lambda g, o: (0, 0)),
                VMEM,
            ]
            + [ANY] * len(held),
            out_specs=[
                pl.BlockSpec((tile, width), place),
                pl.BlockSpec((1, tile, size), lambda g, o: (jnp.maximum(g - 2, 0), 0, 0)),
            ]
            + send_specs,
        ),
        out_shape=[
            jax.ShapeDtypeStruct((rows, width), BF16),
            jax.ShapeDtypeStruct((2, tile, size), F32),
        ]
        + sends,
        input_output_aliases={} if w is None else {6: 0},
        name="weigh_and_sketch",
        cost_estimate=cost(40 * n * tile * width * size, 6 * n * tile * width),
        compiler_params=limit(44),
    )(order, small, totals, totals, ctx_counts, omega, *held)


PACKED = (((0, 0), (0, 1), (0, 2), (0, 3), (3, 3)), ((1, 1), (1, 2), (1, 3), (2, 2), (2, 3)))


def gram_body(parts_of, core, *refs):
    n = sum(len(parts) for parts in parts_of)
    terms, (sketch, sketch_b, own, send) = refs[:n], refs[n : n + 4]
    held, arrival = refs[n + 4 : -1], refs[-1]
    which = [at for parts in parts_of for at in parts]
    copies = [
        pltpu.make_async_copy(terms[i] if at is None else terms[i].at[at], held[i], arrival.at[i])
        for i, at in enumerate(which)
    ]
    for copy in copies:
        copy.start()
    at, i = 0, 0
    for parts in parts_of:
        total = None
        for _ in parts:
            copies[i].wait()
            value = held[i][...].astype(F32)
            total = value if total is None else total + value
            i += 1
        sketch[at : at + total.shape[0], :] = total
        at += total.shape[0]
    sketch_b[...] = sketch[...].astype(BF16)
    size = sketch.shape[1] // 4
    col = lambda i, j: sketch[:, i * size : j * size]
    upper = lambda i, j: dot(col(i, i + 1), col(i, j), ROWS, HIGHEST)
    halves = [
        jnp.concatenate([upper(0, 4), upper(3, 4)], axis=1),
        jnp.concatenate([upper(1, 4), upper(2, 4)], axis=1),
    ]
    for which in range(2):

        @pl.when(core[0] == which)
        def _(which=which):
            own[...] = halves[which]
            send[...] = halves[1 - which]


def gram_of(core, pieces):
    terms = [array for piece in pieces for array, _ in piece]
    parts_of = [[which for _, which in piece] for piece in pieces]
    size = terms[0].shape[-1]
    rows = sum(piece[0][0].shape[-2] for piece in pieces)
    return pl.pallas_call(
        functools.partial(gram_body, parts_of),
        grid=(1,),
        in_specs=[SMEM] + [HBM] * len(terms),
        out_specs=[whole(rows, size)] * 2 + [whole(size // 4, size // 4 * 5)] * 2,
        out_shape=[
            jax.ShapeDtypeStruct((rows, size), F32),
            jax.ShapeDtypeStruct((rows, size), BF16),
            jax.ShapeDtypeStruct((size // 4, size // 4 * 5), F32),
            jax.ShapeDtypeStruct((size // 4, size // 4 * 5), F32),
        ],
        scratch_shapes=[pltpu.VMEM(x.shape[-2:], x.dtype) for x in terms]
        + [pltpu.SemaphoreType.DMA((len(terms),))],
        name="gram",
        cost_estimate=cost(12 * rows * size * size, 8 * rows * size),
        compiler_params=limit(60),
    )(core, *terms)


def small_inverse(g):
    n = len(g)
    g = [list(r) for r in g]
    m = [[None] * n for _ in range(n)]
    out = [[None] * n for _ in range(n)]
    for j in range(0, n, 2):
        k = j + 1
        a, b, c = g[j][j], g[k][j], g[k][k]
        over = 1.0 / (a * c - b * b)
        ca, cb, cc = a * over, b * over, c * over
        ra, rb = lax.rsqrt(a), lax.rsqrt(ca)
        for l in range(j):
            out[j][l] = m[j][l] * ra
            out[k][l] = (ca * m[k][l] - cb * m[j][l]) * rb
        out[j][j], out[k][j], out[k][k] = ra, -cb * rb, ca * rb
        for i in range(k + 1, n):
            f = cc * g[i][j] - cb * g[i][k]
            h = ca * g[i][k] - cb * g[i][j]
            for l in range(k + 1, i + 1):
                g[i][l] = g[i][l] - (f * g[l][j] + h * g[l][k])
            for l in range(j):
                m[i][l] = m[i][l] - (f * m[j][l] + h * m[k][l])
            m[i][j], m[i][k] = -f, -h
    return out


def total(terms):
    while len(terms) > 1:
        terms = [x + y for x, y in zip(terms[::2], terms[1::2])] + terms[len(terms) // 2 * 2 :]
    return terms[0]


def eliminate(tiles, done):
    shape, n, group = tiles[0].shape, len(tiles), 2
    lane = lax.broadcasted_iota(jnp.int32, shape, 1)
    sub = lax.broadcasted_iota(jnp.int32, shape, 0)
    spread = lambda x: jnp.broadcast_to(x, shape)
    columns = lambda x: tuple(spread(x[:, m : m + 1]) for m in range(8))
    pivots = lane < 8

    def turn(t, carry):
        here, tiles = carry
        g = [[spread(here[l][i : i + 1]) for l in range(i + 1)] for i in range(8)]
        rows = [
            jnp.where(pivots, jnp.where(lane == k, 1.0, 0.0), spread(tiles[0][k : k + 1])) for k in range(8)
        ]
        low = small_inverse(g)
        y = [total([low[r][k] * rows[k] for k in range(r + 1)]) for r in range(8)]
        z = [total([low[r][m] * y[r] for r in range(m, 8)]) for m in range(8)]
        new = []
        for x in tiles[1:]:
            x = jnp.where(pivots, 0.0, x) - total([c * w for c, w in zip(columns(x), z)])
            new.append(pltpu.roll(x, NB - 8, 1))
            if len(new) == 1:
                here = columns(new[0])
        final = y[0]
        for r in range(1, 8):
            final = jnp.where(sub == r, y[r], final)
        done[pl.ds(pl.multiple_of(8 * t, 8), 8), :] = final
        return here, tuple(new) + (jnp.zeros(shape, F32),)

    carry = columns(tiles[0]), tuple(tiles)
    for start in range(0, n, group):
        here, tiles = lax.fori_loop(start, start + group, turn, carry)
        carry = here, tiles[: n - start - group]
    return [done[0:8, :]] + [pltpu.roll(done[8 * t : 8 * t + 8, :], 8 * t, 1) for t in range(1, n)]


def factor_body(core, mine, other, out, halves, t, done):
    size = t.shape[0]
    n = size // NB
    block = lambda i: slice(i * NB, (i + 1) * NB)
    halves[core[0]] = mine[...]
    halves[1 - core[0]] = other[...]
    trace = jnp.float32(0.0)
    for half in range(2):
        for at, (i, j) in enumerate(PACKED[half]):
            value = halves[half, :, block(at)]
            t[block(i), block(j)] = value
            if i == j:
                trace = trace + jnp.sum(jnp.where(eye(NB), value, 0.0))
    amount = jnp.float32(0.0001) * trace / jnp.float32(size)
    lower = lax.broadcasted_iota(jnp.int32, (NB, NB), 1) <= lax.broadcasted_iota(jnp.int32, (NB, NB), 0)
    for p in range(n):
        here, before = block(p), slice(0, p * NB)
        diagonal = t[here, here] + jnp.where(eye(NB), amount, 0.0)
        tiles = eliminate([diagonal[8 * i : 8 * i + 8] for i in range(NB // 8)], done)
        inverse = jnp.where(lower, jnp.concatenate(tiles, 0), 0.0)
        out[here, here] = inverse
        if p:
            left = dot(inverse, t[here, before], ((1,), (0,)), HIGHEST)
            out[here, before] = left
        if p < n - 1:
            rest = slice((p + 1) * NB, size)
            out[here, rest] = jnp.zeros((NB, size - (p + 1) * NB), F32)
            right = dot(inverse, t[here, rest], ((1,), (0,)), HIGHEST)
            for q in range(p + 1, n):
                off = (q - p - 1) * NB
                use = right[:, off : off + NB]
                t[block(q), q * NB :] = t[block(q), q * NB :] - dot(use, right[:, off:], ROWS, HIGHEST)
                t[block(q), here] = -dot(use, inverse, ROWS, HIGHEST)
                if p:
                    t[block(q), before] = t[block(q), before] - dot(use, left, ROWS, HIGHEST)


def factor_inverse(core, mine, other):
    size = mine.shape[0] * 4
    return pl.pallas_call(
        factor_body,
        grid=(1,),
        in_specs=[SMEM, whole(*mine.shape), whole(*mine.shape)],
        out_specs=whole(size, size),
        out_shape=jax.ShapeDtypeStruct((size, size), F32),
        scratch_shapes=[
            pltpu.VMEM((2,) + mine.shape, F32),
            pltpu.VMEM((size, size), F32),
            pltpu.VMEM((NB, NB), F32),
        ],
        name="factor_inverse",
        cost_estimate=cost(1, 1),
        compiler_params=limit(24),
    )(core, mine, other)


def basis_body(inverse, sketch, *refs):
    refs[-1][...] = dot(sketch[...], inverse[...], COLS, HIGHEST)


def basis_of(inverse, sketch, tokens):
    rows, size = sketch.shape
    return pl.pallas_call(
        basis_body,
        grid=(1,),
        in_specs=[whole(size, size), whole(rows, size)] + [ANY] * len(tokens),
        out_specs=whole(rows, size),
        out_shape=jax.ShapeDtypeStruct((rows, size), F32),
        name="basis",
        cost_estimate=cost(1, 1),
        compiler_params=limit(24),
    )(inverse, sketch, *tokens)


def turned_body(place, inverse, *refs):
    shares, turned = refs[:-1], refs[-1]
    rows, size = shares[0].shape
    quarter = size // 4
    for i in range(4):
        take = inverse[pl.ds(pl.multiple_of(place[i] * quarter, quarter), quarter), :]
        high = take.astype(BF16)
        low = (take - high.astype(F32)).astype(BF16)
        for d, share in enumerate(shares):
            value = dot(high, share[...], COLS) + dot(low, share[...], COLS)
            start = pl.multiple_of(place[4 + d] * rows, rows)
            turned[i * quarter : (i + 1) * quarter, pl.ds(start, rows)] = value.astype(BF16)


def turned_basis(place, inverse, shares):
    rows, size = shares[0].shape
    n = len(shares)
    return pl.pallas_call(
        turned_body,
        grid=(1,),
        in_specs=[SMEM, whole(size, size)] + [whole(rows, size)] * n,
        out_specs=whole(size, n * rows),
        out_shape=jax.ShapeDtypeStruct((size, n * rows), BF16),
        name="turned_basis",
        cost_estimate=cost(4 * n * rows * size * size, 4 * n * rows * size),
        compiler_params=limit(24),
    )(place, inverse, *shares)


def project_body(turned, w, *refs):
    send, own = refs[-2:]
    half = send.shape[0]
    value = jnp.dot(turned[...], w[...], preferred_element_type=F32)
    send[...] = value[:half].astype(BF16)
    own[...] = value[half:]


def project(turned, w, tokens, start, width, tile):
    size, rows = turned.shape
    steps = width // tile
    first = start // tile
    out = lambda g: (0, g)
    return pl.pallas_call(
        project_body,
        grid=(steps,),
        in_specs=[
            pl.BlockSpec((size, rows), lambda g: (0, 0), pipeline_mode=pl.Buffered(1)),
            pl.BlockSpec((rows, tile), lambda g: (0, first + g)),
        ]
        + [ANY] * len(tokens),
        out_specs=[pl.BlockSpec((size // 2, tile), out), pl.BlockSpec((size // 2, tile), out)],
        out_shape=[
            jax.ShapeDtypeStruct((size // 2, width), BF16),
            jax.ShapeDtypeStruct((size // 2, width), F32),
        ],
        name="project",
        cost_estimate=cost(40 * rows * size * width, 2 * rows * width),
        compiler_params=limit(40),
    )(turned, w, *tokens)


def finish_body(scale, start, mine, core_term, chip_term, *refs):
    out, tick, turned, arrival = refs[-4:]
    tick[...] = jnp.zeros_like(tick)
    total = mine[...] + core_term[...].astype(F32) + chip_term[...].astype(F32)
    turned[...] = jnp.transpose(total * scale)
    copy = pltpu.make_async_copy(turned, out.at[pl.ds(start, turned.shape[0])], arrival)
    copy.start()
    copy.wait()


def finish(own, core_term, chip_term, out, start, full, scale, tokens):
    size, width = chip_term.shape
    held = [] if out is None else [out]
    return pl.pallas_call(
        functools.partial(finish_body, scale, start),
        grid=(1,),
        in_specs=[
            pl.BlockSpec((size, width), lambda g: (1, 0)),
            pl.BlockSpec((size, width), lambda g: (1, 0)),
            whole(size, width),
        ]
        + [ANY] * len(held + tokens),
        out_specs=[ANY, whole(8, NB)],
        out_shape=[jax.ShapeDtypeStruct((full, size), F32), jax.ShapeDtypeStruct((8, NB), F32)],
        input_output_aliases={3: 0} if held else {},
        scratch_shapes=[pltpu.VMEM((width, size), F32), pltpu.SemaphoreType.DMA],
        name="finish",
        cost_estimate=cost(1, 1),
        compiler_params=limit(24),
    )(own, core_term, chip_term, *held, *tokens)


def pass_body(mine, core_term, *refs):
    refs[-1][...] = (mine[...] + core_term[...].astype(F32)).astype(BF16)


def pass_on(own, core_term, tokens):
    size, width = own.shape[0] // 2, own.shape[1]
    return pl.pallas_call(
        pass_body,
        grid=(1,),
        in_specs=[whole(size, width), whole(size, width)] + [ANY] * len(tokens),
        out_specs=whole(size, width),
        out_shape=jax.ShapeDtypeStruct((size, width), BF16),
        name="pass_on",
        cost_estimate=cost(1, 1),
        compiler_params=limit(24),
    )(own, core_term, *tokens)


def rotate(x, n, by):
    return lax.ppermute(x, "col", [(i, (i + by) % n) for i in range(n)])


def swap_col(x, bit):
    return lax.ppermute(x, "col", [(i, i ^ bit) for i in range(4)])


def swap(x, bit):
    return lax.ppermute(x, "row", [(i, i ^ bit) for i in range(4)])


def half_of(x, which):
    rows = x.shape[0] // 2
    return lax.dynamic_slice_in_dim(x, which * rows, rows, 0)


def stack_by(which, mine, other):
    return jnp.where(which == 0, jnp.concatenate([mine, other]), jnp.concatenate([other, mine]))


def pieces_of(share):
    n = share // NB
    return [2 * NB] * ((n - 2) // 2) + [NB] * (n - (n - 2) // 2 * 2) if n > 2 else [NB] * n


def sketch_phase(counts, ctx_counts, omega, col):
    rows, width = counts.shape
    ctx_counts = ctx_counts.reshape(1, width)
    totals, small = row_sums(counts, ctx_counts)
    totals = totals + swap_col(totals, 1)
    totals = totals + swap_col(totals, 2)
    order = jnp.stack([col ^ 1, col ^ 3, col ^ 2, col])
    tiles = pieces_of(rows // 4)
    w, offset, pieces, passed, arrived = None, 0, [], [], []
    for k, tile in enumerate(tiles):
        last = k == len(tiles) - 1
        tokens = passed[k - 2 : k - 1] if k >= 2 else []
        tokens = tokens + (arrived[k - 3 : k - 2] if k >= 3 else [])
        w, keep, *sends = weigh(small, totals, ctx_counts, omega, w, order, offset, tile, tokens, last)
        offset += tile
        if last:
            theirs, mine = swap_col(sends[1], 1), swap_col(sends[0], 1)
            passed.append(pass_on(keep.reshape(2 * tile, -1), theirs, arrived[: max(0, k - 1)]))
            mine = (mine, None)
        else:
            near = swap_col(sends[0], 1)
            passed.append((keep[0] + near[1].astype(F32)).astype(BF16))
            mine = (near, 0)
        arrived.append(swap_col(passed[k], 2))
        pieces.append([(keep, 1), mine, (arrived[k], None)])
    return w, pieces


def sketch_phase_any(counts, ctx_counts, omega, col):
    row_part = jnp.sum(counts.astype(F32), axis=1)
    ctx_weight = ctx_counts.astype(F32) ** 0.75
    log_ctx = jnp.log(ctx_weight)[None, :]
    row_total, ctx_total = lax.psum((row_part, jnp.sum(ctx_weight)), "col")
    value = jnp.log(counts.astype(F32)) + (
        jnp.log(ctx_total) - jnp.log(F32(5.0)) - jnp.log(row_total)[:, None] - log_ctx
    )
    w = jnp.maximum(value, 0.0).astype(BF16)
    partial = jnp.dot(w, omega, preferred_element_type=F32)
    return w, [[(lax.psum_scatter(partial, "col", scatter_dimension=0, tiled=True), None)]]


def shards(counts, ctx_counts, omega):
    rows, width = counts.shape
    n = lax.axis_size("col")
    row = lax.axis_index("row")
    col = lax.axis_index("col")
    core, chip = row % 2, row // 2
    direct = n == 4 and rows % (4 * NB) == 0
    phase = sketch_phase if direct else sketch_phase_any
    w, pieces = phase(counts, ctx_counts, omega, col)
    sketch, sketch_b, half, other_half = gram_of(core.reshape(1), pieces)
    half = half + swap(other_half, 1)
    quarter = half_of(half, chip) + swap(half_of(half, 1 - chip), 2)
    if direct:
        quarter = quarter + swap_col(quarter, 1)
        quarter = quarter + swap_col(quarter, 2)
        shares = [sketch_b] + [rotate(sketch_b, n, d) for d in range(1, n)]
        sources = [(col - d) % n for d in range(n)]
    else:
        quarter = lax.psum(quarter, "col")
        shares = [lax.all_gather(sketch_b, "col", tiled=True)]
        sources = [jnp.int32(0)]
    half = stack_by(chip, quarter, swap(quarter, 2))
    inverse = factor_inverse(core.reshape(1), half, swap(half, 1))
    place = jnp.stack([row ^ 3, row ^ 1, row ^ 2, row] + sources)
    turned = turned_basis(place, inverse, shares)
    widths = (1, 2, 3, 3, 4, 2, 1) if width % (16 * NB) == 0 else (1,) * 8
    unit = width // sum(widths)
    scale = float(1.0 / (rows * lax.axis_size("row")) ** 0.5)
    quarter = omega.shape[1] // 4
    out, start = None, 0
    sent, passed, arrived, ended = [], [], [], []
    terms = []

    def end(tokens):
        j = len(ended)
        out = ended[-1][0] if ended else None
        ended.append(finish(*terms[j][:2], arrived[j], out, terms[j][2], width, scale, tokens))

    for j, pieces in enumerate(widths):
        piece = pieces * unit
        tokens = sent[-1:] + (passed[-2:-1] if j >= 2 else []) + (arrived[-3:-2] if j >= 3 else [])
        send, mine = project(turned, w, tokens, start, piece, unit)
        sent.append(send)
        core_term = swap(send, 1)
        if j == len(widths) - 1:
            basis = basis_of(inverse, sketch, [send])
            for _ in range(3):
                end([])
            chip_send = pass_on(mine, core_term, [arrived[-2], basis, ended[-1][1]])
        else:
            chip_send = (mine[:quarter] + core_term[:quarter].astype(F32)).astype(BF16)
        passed.append(chip_send)
        arrived.append(swap(chip_send, 2))
        terms.append((mine, core_term, start))
        start += piece
    while len(ended) < len(widths):
        end([])
    out = ended[-1][0]
    return (basis, out)


def solution(mesh):
    in_specs = (P(("grp", "row"), "col"), P(("grp", "col")), P("col", None))
    out_specs = (P(("grp", "row", "col"), None), P(("grp", "col"), "row"))
    return jax.shard_map(shards, mesh=mesh, in_specs=in_specs, out_specs=out_specs, check_vma=False)
```

```python
import functools

import jax
import jax.numpy as jnp
from jax import lax
from jax.experimental import pallas as pl
from jax.experimental.pallas import tpu as pltpu
from jax.sharding import PartitionSpec as P

HIGHEST = lax.Precision.HIGHEST
F32 = jnp.float32
BF16 = jnp.bfloat16
NB = 128
ROWS = ((0,), (0,))
COLS = ((1,), (1,))
VMEM = pl.BlockSpec(memory_space=pltpu.VMEM)
SMEM = pl.BlockSpec(memory_space=pltpu.SMEM)
ANY = pl.BlockSpec(memory_space=pl.ANY)
HBM = pl.BlockSpec(memory_space=pltpu.HBM)


def limit(mib):
    return pltpu.CompilerParams(vmem_limit_bytes=mib * 1024 * 1024)


def cost(flops, nbytes):
    return pl.CostEstimate(flops=int(flops), bytes_accessed=int(nbytes), transcendentals=0)


def whole(*shape):
    return pl.BlockSpec(shape, lambda *_: (0,) * len(shape))


def dot(a, b, contract, precision=None):
    return lax.dot_general(a, b, (contract, ((), ())), precision=precision, preferred_element_type=F32)


def eye(n):
    return lax.broadcasted_iota(jnp.int32, (n, n), 0) == lax.broadcasted_iota(jnp.int32, (n, n), 1)


def totals_body(counts, ctx_counts, out, small):
    tile, width = counts.shape
    n = tile // NB
    step = pl.program_id(0)
    for at in range(n):
        parts = []
        for r in range(at * NB, (at + 1) * NB, 32):
            acc = None
            for c in range(0, width, NB):
                value = counts[r : r + 32, c : c + NB]
                small[r : r + 32, c : c + NB] = (value - 128).astype(jnp.int8)
                acc = value if acc is None else acc + value
            parts.append(jnp.sum(acc.astype(F32), axis=1, keepdims=True))
        column = jnp.concatenate(parts, 0)
        out[step * n + at] = jnp.sum(jnp.where(eye(NB), column, 0.0), axis=0, keepdims=True)

    @pl.when(step == 0)
    def _():
        count = ctx_counts[...].astype(F32)
        weight = jnp.sqrt(count) * jnp.sqrt(jnp.sqrt(count))
        out[out.shape[0] - 1] = jnp.broadcast_to(jnp.sum(weight, axis=1, keepdims=True), (1, NB))


def row_sums(counts, ctx_counts):
    rows, width = counts.shape
    tile = 2 * NB
    return pl.pallas_call(
        totals_body,
        grid=(rows // tile,),
        in_specs=[pl.BlockSpec((tile, width), lambda g: (g, 0)), whole(1, width)],
        out_specs=[whole(rows // NB + 1, 1, NB), pl.BlockSpec((tile, width), lambda g: (g, 0))],
        out_shape=[
            jax.ShapeDtypeStruct((rows // NB + 1, 1, NB), F32),
            jax.ShapeDtypeStruct((rows, width), jnp.int8),
        ],
        name="row_sums",
        cost_estimate=cost(2000 * rows * width, 1),
        compiler_params=limit(45),
    )(counts, ctx_counts)


def weigh_body(split, order, small, row_total, ctx_total, ctx_counts, omega, *refs):
    w, keep, *sends = refs[-4:] if split else refs[-3:]
    tile, width = w.shape
    step = min(2048, width)
    row_log = [jnp.log(ctx_total[0]) - jnp.log(F32(5.0)) - jnp.log(row_total[i]) for i in range(tile // NB)]
    column = jnp.concatenate([jnp.sum(jnp.where(eye(NB), x, 0.0), axis=1, keepdims=True) for x in row_log])
    log_ctx = 0.75 * jnp.log(ctx_counts[...].astype(F32))
    acc = jnp.zeros((tile, omega.shape[1]), F32)
    for c in range(0, width, step):
        here = slice(c, c + step)
        for r in range(0, tile, 32):
            rows = slice(r, r + 32)
            count = small[rows, here].astype(F32) + 128.0
            value = jnp.log(count) + (column[rows] - log_ctx[:, here])
            w[rows, here] = jnp.maximum(value, 0.0).astype(BF16)
        acc = acc + jnp.dot(w[:, here], omega[here, :], preferred_element_type=F32)

    if split:
        for g in range(2):

            @pl.when(pl.program_id(0) == g)
            def _(g=g):
                sends[g][...] = acc.astype(BF16)

    else:

        @pl.when(pl.program_id(0) < 2)
        def _():
            sends[0][0] = acc.astype(BF16)

    @pl.when(pl.program_id(0) >= 2)
    def _():
        keep[0] = acc


def weigh(small, totals, ctx_counts, omega, w, order, offset, tile, tokens, split):
    n = order.shape[0]
    rows, width = small.shape
    size = omega.shape[1]
    share = rows // n
    place = lambda g, o: (o[g] * (share // tile) + offset // tile, 0)
    held = ([] if w is None else [w]) + tokens
    if split:
        sends = [jax.ShapeDtypeStruct((tile, size), BF16)] * 2
        send_specs = [whole(tile, size)] * 2
    else:
        sends = [jax.ShapeDtypeStruct((2, tile, size), BF16)]
        send_specs = [pl.BlockSpec((1, tile, size), lambda g, o: (jnp.minimum(g, 1), 0, 0))]
    return pl.pallas_call(
        functools.partial(weigh_body, split),
        grid_spec=pltpu.PrefetchScalarGridSpec(
            num_scalar_prefetch=1,
            grid=(n,),
            in_specs=[
                pl.BlockSpec((tile, width), place),
                pl.BlockSpec((tile // NB, 1, NB), lambda g, o: place(g, o) + (0,)),
                pl.BlockSpec((1, 1, NB), lambda g, o: (rows // NB, 0, 0)),
                pl.BlockSpec((1, width), lambda g, o: (0, 0)),
                VMEM,
            ]
            + [ANY] * len(held),
            out_specs=[
                pl.BlockSpec((tile, width), place),
                pl.BlockSpec((1, tile, size), lambda g, o: (jnp.maximum(g - 2, 0), 0, 0)),
            ]
            + send_specs,
        ),
        out_shape=[
            jax.ShapeDtypeStruct((rows, width), BF16),
            jax.ShapeDtypeStruct((2, tile, size), F32),
        ]
        + sends,
        input_output_aliases={} if w is None else {6: 0},
        name="weigh_and_sketch",
        cost_estimate=cost(40 * n * tile * width * size, 6 * n * tile * width),
        compiler_params=limit(44),
    )(order, small, totals, totals, ctx_counts, omega, *held)


PACKED = (((0, 0), (0, 1), (0, 2), (0, 3), (3, 3)), ((1, 1), (1, 2), (1, 3), (2, 2), (2, 3)))


def gram_body(parts_of, core, *refs):
    n = sum(len(parts) for parts in parts_of)
    terms, (sketch, sketch_b, own, send) = refs[:n], refs[n : n + 4]
    held, arrival = refs[n + 4 : -1], refs[-1]
    which = [at for parts in parts_of for at in parts]
    copies = [
        pltpu.make_async_copy(terms[i] if at is None else terms[i].at[at], held[i], arrival.at[i])
        for i, at in enumerate(which)
    ]
    for copy in copies:
        copy.start()
    at, i = 0, 0
    for parts in parts_of:
        total = None
        for _ in parts:
            copies[i].wait()
            value = held[i][...].astype(F32)
            total = value if total is None else total + value
            i += 1
        sketch[at : at + total.shape[0], :] = total
        at += total.shape[0]
    sketch_b[...] = sketch[...].astype(BF16)
    size = sketch.shape[1] // 4
    col = lambda i, j: sketch[:, i * size : j * size]
    upper = lambda i, j: dot(col(i, i + 1), col(i, j), ROWS, HIGHEST)
    halves = [
        jnp.concatenate([upper(0, 4), upper(3, 4)], axis=1),
        jnp.concatenate([upper(1, 4), upper(2, 4)], axis=1),
    ]
    for which in range(2):

        @pl.when(core[0] == which)
        def _(which=which):
            own[...] = halves[which]
            send[...] = halves[1 - which]


def gram_of(core, pieces):
    terms = [array for piece in pieces for array, _ in piece]
    parts_of = [[which for _, which in piece] for piece in pieces]
    size = terms[0].shape[-1]
    rows = sum(piece[0][0].shape[-2] for piece in pieces)
    return pl.pallas_call(
        functools.partial(gram_body, parts_of),
        grid=(1,),
        in_specs=[SMEM] + [HBM] * len(terms),
        out_specs=[whole(rows, size)] * 2 + [whole(size // 4, size // 4 * 5)] * 2,
        out_shape=[
            jax.ShapeDtypeStruct((rows, size), F32),
            jax.ShapeDtypeStruct((rows, size), BF16),
            jax.ShapeDtypeStruct((size // 4, size // 4 * 5), F32),
            jax.ShapeDtypeStruct((size // 4, size // 4 * 5), F32),
        ],
        scratch_shapes=[pltpu.VMEM(x.shape[-2:], x.dtype) for x in terms]
        + [pltpu.SemaphoreType.DMA((len(terms),))],
        name="gram",
        cost_estimate=cost(12 * rows * size * size, 8 * rows * size),
        compiler_params=limit(60),
    )(core, *terms)


def small_inverse(g):
    n = len(g)
    g = [list(r) for r in g]
    m = [[None] * n for _ in range(n)]
    out = [[None] * n for _ in range(n)]
    for j in range(0, n, 2):
        k = j + 1
        a, b, c = g[j][j], g[k][j], g[k][k]
        over = 1.0 / (a * c - b * b)
        ca, cb, cc = a * over, b * over, c * over
        ra, rb = lax.rsqrt(a), lax.rsqrt(ca)
        for l in range(j):
            out[j][l] = m[j][l] * ra
            out[k][l] = (ca * m[k][l] - cb * m[j][l]) * rb
        out[j][j], out[k][j], out[k][k] = ra, -cb * rb, ca * rb
        for i in range(k + 1, n):
            f = cc * g[i][j] - cb * g[i][k]
            h = ca * g[i][k] - cb * g[i][j]
            for l in range(k + 1, i + 1):
                g[i][l] = g[i][l] - (f * g[l][j] + h * g[l][k])
            for l in range(j):
                m[i][l] = m[i][l] - (f * m[j][l] + h * m[k][l])
            m[i][j], m[i][k] = -f, -h
    return out


def total(terms):
    while len(terms) > 1:
        terms = [x + y for x, y in zip(terms[::2], terms[1::2])] + terms[len(terms) // 2 * 2 :]
    return terms[0]


def eliminate(tiles, done):
    shape, n, group = tiles[0].shape, len(tiles), 2
    lane = lax.broadcasted_iota(jnp.int32, shape, 1)
    sub = lax.broadcasted_iota(jnp.int32, shape, 0)
    spread = lambda x: jnp.broadcast_to(x, shape)
    columns = lambda x: tuple(spread(x[:, m : m + 1]) for m in range(8))
    pivots = lane < 8

    def turn(t, carry):
        here, tiles = carry
        g = [[spread(here[l][i : i + 1]) for l in range(i + 1)] for i in range(8)]
        rows = [
            jnp.where(pivots, jnp.where(lane == k, 1.0, 0.0), spread(tiles[0][k : k + 1])) for k in range(8)
        ]
        low = small_inverse(g)
        y = [total([low[r][k] * rows[k] for k in range(r + 1)]) for r in range(8)]
        z = [total([low[r][m] * y[r] for r in range(m, 8)]) for m in range(8)]
        new = []
        for x in tiles[1:]:
            x = jnp.where(pivots, 0.0, x) - total([c * w for c, w in zip(columns(x), z)])
            new.append(pltpu.roll(x, NB - 8, 1))
            if len(new) == 1:
                here = columns(new[0])
        final = y[0]
        for r in range(1, 8):
            final = jnp.where(sub == r, y[r], final)
        done[pl.ds(pl.multiple_of(8 * t, 8), 8), :] = final
        return here, tuple(new) + (jnp.zeros(shape, F32),)

    carry = columns(tiles[0]), tuple(tiles)
    for start in range(0, n, group):
        here, tiles = lax.fori_loop(start, start + group, turn, carry)
        carry = here, tiles[: n - start - group]
    return [done[0:8, :]] + [pltpu.roll(done[8 * t : 8 * t + 8, :], 8 * t, 1) for t in range(1, n)]


def factor_body(core, mine, other, out, halves, t, done):
    size = t.shape[0]
    n = size // NB
    block = lambda i: slice(i * NB, (i + 1) * NB)
    halves[core[0]] = mine[...]
    halves[1 - core[0]] = other[...]
    trace = jnp.float32(0.0)
    for half in range(2):
        for at, (i, j) in enumerate(PACKED[half]):
            value = halves[half, :, block(at)]
            t[block(i), block(j)] = value
            if i == j:
                trace = trace + jnp.sum(jnp.where(eye(NB), value, 0.0))
    amount = jnp.float32(0.0001) * trace / jnp.float32(size)
    lower = lax.broadcasted_iota(jnp.int32, (NB, NB), 1) <= lax.broadcasted_iota(jnp.int32, (NB, NB), 0)
    for p in range(n):
        here, before = block(p), slice(0, p * NB)
        diagonal = t[here, here] + jnp.where(eye(NB), amount, 0.0)
        tiles = eliminate([diagonal[8 * i : 8 * i + 8] for i in range(NB // 8)], done)
        inverse = jnp.where(lower, jnp.concatenate(tiles, 0), 0.0)
        out[here, here] = inverse
        if p:
            left = dot(inverse, t[here, before], ((1,), (0,)), HIGHEST)
            out[here, before] = left
        if p < n - 1:
            rest = slice((p + 1) * NB, size)
            out[here, rest] = jnp.zeros((NB, size - (p + 1) * NB), F32)
            right = dot(inverse, t[here, rest], ((1,), (0,)), HIGHEST)
            for q in range(p + 1, n):
                off = (q - p - 1) * NB
                use = right[:, off : off + NB]
                t[block(q), q * NB :] = t[block(q), q * NB :] - dot(use, right[:, off:], ROWS, HIGHEST)
                t[block(q), here] = -dot(use, inverse, ROWS, HIGHEST)
                if p:
                    t[block(q), before] = t[block(q), before] - dot(use, left, ROWS, HIGHEST)


def factor_inverse(core, mine, other):
    size = mine.shape[0] * 4
    return pl.pallas_call(
        factor_body,
        grid=(1,),
        in_specs=[SMEM, whole(*mine.shape), whole(*mine.shape)],
        out_specs=whole(size, size),
        out_shape=jax.ShapeDtypeStruct((size, size), F32),
        scratch_shapes=[
            pltpu.VMEM((2,) + mine.shape, F32),
            pltpu.VMEM((size, size), F32),
            pltpu.VMEM((NB, NB), F32),
        ],
        name="factor_inverse",
        cost_estimate=cost(1, 1),
        compiler_params=limit(24),
    )(core, mine, other)


def basis_body(inverse, sketch, *refs):
    refs[-1][...] = dot(sketch[...], inverse[...], COLS, HIGHEST)


def basis_of(inverse, sketch, tokens):
    rows, size = sketch.shape
    return pl.pallas_call(
        basis_body,
        grid=(1,),
        in_specs=[whole(size, size), whole(rows, size)] + [ANY] * len(tokens),
        out_specs=whole(rows, size),
        out_shape=jax.ShapeDtypeStruct((rows, size), F32),
        name="basis",
        cost_estimate=cost(1, 1),
        compiler_params=limit(24),
    )(inverse, sketch, *tokens)


def turned_body(n, place, inverse, *refs):
    shares, (turned, high, low) = refs[:n], refs[-3:]
    size = inverse.shape[0]
    quarter = size // 4
    step = pl.program_id(0)

    @pl.when(step == 0)
    def _():
        for i in range(4):
            rows = slice(i * quarter, (i + 1) * quarter)
            take = inverse[pl.ds(pl.multiple_of(place[i] * quarter, quarter), quarter), :]
            high[rows, :] = take.astype(BF16)
            low[rows, :] = (take - take.astype(BF16).astype(F32)).astype(BF16)

    for d in range(n):

        @pl.when(step == d)
        def _(d=d):
            value = dot(high[...], shares[d][...], COLS) + dot(low[...], shares[d][...], COLS)
            turned[...] = value.astype(BF16)


def turned_basis(place, inverse, shares, held, first, n_all):
    rows, size = shares[0].shape
    n = len(shares)
    held = [] if held is None else [held]
    return pl.pallas_call(
        functools.partial(turned_body, n),
        grid_spec=pltpu.PrefetchScalarGridSpec(
            num_scalar_prefetch=1,
            grid=(n,),
            in_specs=[whole(size, size)] + [whole(rows, size)] * n + [ANY] * len(held),
            out_specs=pl.BlockSpec((size, rows), lambda g, p: (0, p[4 + first + g])),
            scratch_shapes=[pltpu.VMEM((size, size), BF16)] * 2,
        ),
        out_shape=jax.ShapeDtypeStruct((size, n_all * rows), BF16),
        input_output_aliases={2 + n: 0} if held else {},
        name="turned_basis",
        cost_estimate=cost(4 * n * rows * size * size, 4 * n * rows * size),
        compiler_params=limit(24),
    )(place, inverse, *shares, *held)


def project_body(turned, w, *refs):
    send, own = refs[-2:]
    half = send.shape[0]
    value = jnp.dot(turned[...], w[...], preferred_element_type=F32)
    send[...] = value[:half].astype(BF16)
    own[...] = value[half:]


def project(turned, w, tokens, start, width, tile):
    size, rows = turned.shape
    steps = width // tile
    first = start // tile
    out = lambda g: (0, g)
    return pl.pallas_call(
        project_body,
        grid=(steps,),
        in_specs=[
            pl.BlockSpec((size, rows), lambda g: (0, 0), pipeline_mode=pl.Buffered(1)),
            pl.BlockSpec((rows, tile), lambda g: (0, first + g)),
        ]
        + [ANY] * len(tokens),
        out_specs=[pl.BlockSpec((size // 2, tile), out), pl.BlockSpec((size // 2, tile), out)],
        out_shape=[
            jax.ShapeDtypeStruct((size // 2, width), BF16),
            jax.ShapeDtypeStruct((size // 2, width), F32),
        ],
        name="project",
        cost_estimate=cost(40 * rows * size * width, 2 * rows * width),
        compiler_params=limit(34),
    )(turned, w, *tokens)


def finish_body(scale, start, mine, core_term, chip_term, *refs):
    out, tick, turned, arrival = refs[-4:]
    tick[...] = jnp.zeros_like(tick)
    total = mine[...] + core_term[...].astype(F32) + chip_term[...].astype(F32)
    turned[...] = jnp.transpose(total * scale)
    copy = pltpu.make_async_copy(turned, out.at[pl.ds(start, turned.shape[0])], arrival)
    copy.start()
    copy.wait()


def finish(own, core_term, chip_term, out, start, full, scale, tokens):
    size, width = chip_term.shape
    held = [] if out is None else [out]
    return pl.pallas_call(
        functools.partial(finish_body, scale, start),
        grid=(1,),
        in_specs=[
            pl.BlockSpec((size, width), lambda g: (1, 0)),
            pl.BlockSpec((size, width), lambda g: (1, 0)),
            whole(size, width),
        ]
        + [ANY] * len(held + tokens),
        out_specs=[ANY, whole(8, NB)],
        out_shape=[jax.ShapeDtypeStruct((full, size), F32), jax.ShapeDtypeStruct((8, NB), F32)],
        input_output_aliases={3: 0} if held else {},
        scratch_shapes=[pltpu.VMEM((width, size), F32), pltpu.SemaphoreType.DMA],
        name="finish",
        cost_estimate=cost(1, 1),
        compiler_params=limit(24),
    )(own, core_term, chip_term, *held, *tokens)


def pass_body(mine, core_term, *refs):
    refs[-1][...] = (mine[...] + core_term[...].astype(F32)).astype(BF16)


def pass_on(own, core_term, tokens):
    size, width = own.shape[0] // 2, own.shape[1]
    return pl.pallas_call(
        pass_body,
        grid=(1,),
        in_specs=[whole(size, width), whole(size, width)] + [ANY] * len(tokens),
        out_specs=whole(size, width),
        out_shape=jax.ShapeDtypeStruct((size, width), BF16),
        name="pass_on",
        cost_estimate=cost(1, 1),
        compiler_params=limit(24),
    )(own, core_term, *tokens)


def rotate(x, n, by):
    return lax.ppermute(x, "col", [(i, (i + by) % n) for i in range(n)])


def swap_col(x, bit):
    return lax.ppermute(x, "col", [(i, i ^ bit) for i in range(4)])


def swap(x, bit):
    return lax.ppermute(x, "row", [(i, i ^ bit) for i in range(4)])


def half_of(x, which):
    rows = x.shape[0] // 2
    return lax.dynamic_slice_in_dim(x, which * rows, rows, 0)


def stack_by(which, mine, other):
    return jnp.where(which == 0, jnp.concatenate([mine, other]), jnp.concatenate([other, mine]))


def pieces_of(share):
    n = share // NB
    return [2 * NB] * ((n - 2) // 2) + [NB] * (n - (n - 2) // 2 * 2) if n > 2 else [NB] * n


def sketch_phase(counts, ctx_counts, omega, col):
    rows, width = counts.shape
    ctx_counts = ctx_counts.reshape(1, width)
    totals, small = row_sums(counts, ctx_counts)
    totals = totals + swap_col(totals, 1)
    totals = totals + swap_col(totals, 2)
    order = jnp.stack([col ^ 1, col ^ 3, col ^ 2, col])
    tiles = pieces_of(rows // 4)
    w, offset, pieces, passed, arrived = None, 0, [], [], []
    for k, tile in enumerate(tiles):
        last = k == len(tiles) - 1
        tokens = passed[k - 2 : k - 1] if k >= 2 else []
        tokens = tokens + (arrived[k - 3 : k - 2] if k >= 3 else [])
        w, keep, *sends = weigh(small, totals, ctx_counts, omega, w, order, offset, tile, tokens, last)
        offset += tile
        if last:
            theirs, mine = swap_col(sends[1], 1), swap_col(sends[0], 1)
            passed.append(pass_on(keep.reshape(2 * tile, -1), theirs, arrived[: max(0, k - 1)]))
            mine = (mine, None)
        else:
            near = swap_col(sends[0], 1)
            passed.append((keep[0] + near[1].astype(F32)).astype(BF16))
            mine = (near, 0)
        arrived.append(swap_col(passed[k], 2))
        pieces.append([(keep, 1), mine, (arrived[k], None)])
    return w, pieces


def sketch_phase_any(counts, ctx_counts, omega, col):
    row_part = jnp.sum(counts.astype(F32), axis=1)
    ctx_weight = ctx_counts.astype(F32) ** 0.75
    log_ctx = jnp.log(ctx_weight)[None, :]
    row_total, ctx_total = lax.psum((row_part, jnp.sum(ctx_weight)), "col")
    value = jnp.log(counts.astype(F32)) + (
        jnp.log(ctx_total) - jnp.log(F32(5.0)) - jnp.log(row_total)[:, None] - log_ctx
    )
    w = jnp.maximum(value, 0.0).astype(BF16)
    partial = jnp.dot(w, omega, preferred_element_type=F32)
    return w, [[(lax.psum_scatter(partial, "col", scatter_dimension=0, tiled=True), None)]]


def shards(counts, ctx_counts, omega):
    rows, width = counts.shape
    n = lax.axis_size("col")
    row = lax.axis_index("row")
    col = lax.axis_index("col")
    core, chip = row % 2, row // 2
    direct = n == 4 and rows % (4 * NB) == 0
    phase = sketch_phase if direct else sketch_phase_any
    w, pieces = phase(counts, ctx_counts, omega, col)
    sketch, sketch_b, half, other_half = gram_of(core.reshape(1), pieces)
    half = half + swap(other_half, 1)
    quarter = half_of(half, chip) + swap(half_of(half, 1 - chip), 2)
    if direct:
        quarter = quarter + swap_col(quarter, 1)
        quarter = quarter + swap_col(quarter, 2)
        shares = [sketch_b] + [rotate(sketch_b, n, d) for d in (1, 2, 3)]
        sources = [(col - d) % n for d in range(n)]
    else:
        quarter = lax.psum(quarter, "col")
        shares = [lax.all_gather(sketch_b, "col", tiled=True)]
        sources = [jnp.int32(0)]
    half = stack_by(chip, quarter, swap(quarter, 2))
    inverse = factor_inverse(core.reshape(1), half, swap(half, 1))
    place = jnp.stack([row ^ 3, row ^ 1, row ^ 2, row] + sources)
    n_share = len(shares)
    first = (n_share + 1) // 2
    turned = turned_basis(place, inverse, shares[:first], None, 0, n_share)
    if n_share > 1:
        turned = turned_basis(place, inverse, shares[first:], turned, first, n_share)
    widths = (1, 2, 3, 3, 4, 2, 1) if width % (16 * NB) == 0 else (1,) * 8
    unit = width // sum(widths)
    scale = float(1.0 / (rows * lax.axis_size("row")) ** 0.5)
    quarter = omega.shape[1] // 4
    out, start = None, 0
    sent, passed, arrived, ended = [], [], [], []
    terms = []

    def end(tokens):
        j = len(ended)
        out = ended[-1][0] if ended else None
        ended.append(finish(*terms[j][:2], arrived[j], out, terms[j][2], width, scale, tokens))

    for j, pieces in enumerate(widths):
        piece = pieces * unit
        tokens = sent[-1:] + (passed[-2:-1] if j >= 2 else []) + (arrived[-3:-2] if j >= 3 else [])
        send, mine = project(turned, w, tokens, start, piece, unit)
        sent.append(send)
        core_term = swap(send, 1)
        if j == len(widths) - 1:
            basis = basis_of(inverse, sketch, [send])
            for _ in range(3):
                end([])
            chip_send = pass_on(mine, core_term, [arrived[-2], basis, ended[-1][1]])
        else:
            chip_send = (mine[:quarter] + core_term[:quarter].astype(F32)).astype(BF16)
        passed.append(chip_send)
        arrived.append(swap(chip_send, 2))
        terms.append((mine, core_term, start))
        start += piece
    while len(ended) < len(widths):
        end([])
    out = ended[-1][0]
    return (basis, out)


def solution(mesh):
    in_specs = (P(("grp", "row"), "col"), P(("grp", "col")), P("col", None))
    out_specs = (P(("grp", "row", "col"), None), P(("grp", "col"), "row"))
    return jax.shard_map(shards, mesh=mesh, in_specs=in_specs, out_specs=out_specs, check_vma=False)
```

```python
import functools

import jax
import jax.numpy as jnp
from jax import lax
from jax.experimental import pallas as pl
from jax.experimental.pallas import tpu as pltpu
from jax.sharding import PartitionSpec as P

HIGHEST = lax.Precision.HIGHEST
F32 = jnp.float32
BF16 = jnp.bfloat16
NB = 128
ROWS = ((0,), (0,))
COLS = ((1,), (1,))
VMEM = pl.BlockSpec(memory_space=pltpu.VMEM)
SMEM = pl.BlockSpec(memory_space=pltpu.SMEM)
ANY = pl.BlockSpec(memory_space=pl.ANY)
HBM = pl.BlockSpec(memory_space=pltpu.HBM)


def limit(mib):
    return pltpu.CompilerParams(vmem_limit_bytes=mib * 1024 * 1024)


def cost(flops, nbytes):
    return pl.CostEstimate(flops=int(flops), bytes_accessed=int(nbytes), transcendentals=0)


def whole(*shape):
    return pl.BlockSpec(shape, lambda *_: (0,) * len(shape))


def dot(a, b, contract, precision=None):
    return lax.dot_general(a, b, (contract, ((), ())), precision=precision, preferred_element_type=F32)


def eye(n):
    return lax.broadcasted_iota(jnp.int32, (n, n), 0) == lax.broadcasted_iota(jnp.int32, (n, n), 1)


def totals_body(counts, ctx_counts, out, small):
    tile, width = counts.shape
    n = tile // NB
    step = pl.program_id(0)
    for at in range(n):
        parts = []
        for r in range(at * NB, (at + 1) * NB, 32):
            acc = None
            for c in range(0, width, NB):
                value = counts[r : r + 32, c : c + NB]
                small[r : r + 32, c : c + NB] = (value - 128).astype(jnp.int8)
                acc = value if acc is None else acc + value
            parts.append(jnp.sum(acc.astype(F32), axis=1, keepdims=True))
        column = jnp.concatenate(parts, 0)
        out[step * n + at] = jnp.sum(jnp.where(eye(NB), column, 0.0), axis=0, keepdims=True)

    @pl.when(step == 0)
    def _():
        count = ctx_counts[...].astype(F32)
        weight = jnp.sqrt(count) * jnp.sqrt(jnp.sqrt(count))
        out[out.shape[0] - 1] = jnp.broadcast_to(jnp.sum(weight, axis=1, keepdims=True), (1, NB))


def row_sums(counts, ctx_counts):
    rows, width = counts.shape
    tile = 2 * NB
    return pl.pallas_call(
        totals_body,
        grid=(rows // tile,),
        in_specs=[pl.BlockSpec((tile, width), lambda g: (g, 0)), whole(1, width)],
        out_specs=[whole(rows // NB + 1, 1, NB), pl.BlockSpec((tile, width), lambda g: (g, 0))],
        out_shape=[
            jax.ShapeDtypeStruct((rows // NB + 1, 1, NB), F32),
            jax.ShapeDtypeStruct((rows, width), jnp.int8),
        ],
        name="row_sums",
        cost_estimate=cost(2000 * rows * width, 1),
        compiler_params=limit(45),
    )(counts, ctx_counts)


def weigh_body(split, order, small, row_total, ctx_total, ctx_counts, omega, *refs):
    w, keep, *sends = refs[-4:] if split else refs[-3:]
    tile, width = w.shape
    step = min(2048, width)
    row_log = [jnp.log(ctx_total[0]) - jnp.log(F32(5.0)) - jnp.log(row_total[i]) for i in range(tile // NB)]
    column = jnp.concatenate([jnp.sum(jnp.where(eye(NB), x, 0.0), axis=1, keepdims=True) for x in row_log])
    log_ctx = 0.75 * jnp.log(ctx_counts[...].astype(F32))
    acc = jnp.zeros((tile, omega.shape[1]), F32)
    for c in range(0, width, step):
        here = slice(c, c + step)
        for r in range(0, tile, 32):
            rows = slice(r, r + 32)
            count = small[rows, here].astype(F32) + 128.0
            value = jnp.log(count) + (column[rows] - log_ctx[:, here])
            w[rows, here] = jnp.maximum(value, 0.0).astype(BF16)
        acc = acc + jnp.dot(w[:, here], omega[here, :], preferred_element_type=F32)

    if split:
        for g in range(2):

            @pl.when(pl.program_id(0) == g)
            def _(g=g):
                sends[g][...] = acc.astype(BF16)

    else:

        @pl.when(pl.program_id(0) < 2)
        def _():
            sends[0][0] = acc.astype(BF16)

    @pl.when(pl.program_id(0) >= 2)
    def _():
        keep[0] = acc


def weigh(small, totals, ctx_counts, omega, w, order, offset, tile, tokens, split):
    n = order.shape[0]
    rows, width = small.shape
    size = omega.shape[1]
    share = rows // n
    place = lambda g, o: (o[g] * (share // tile) + offset // tile, 0)
    held = ([] if w is None else [w]) + tokens
    if split:
        sends = [jax.ShapeDtypeStruct((tile, size), BF16)] * 2
        send_specs = [whole(tile, size)] * 2
    else:
        sends = [jax.ShapeDtypeStruct((2, tile, size), BF16)]
        send_specs = [pl.BlockSpec((1, tile, size), lambda g, o: (jnp.minimum(g, 1), 0, 0))]
    return pl.pallas_call(
        functools.partial(weigh_body, split),
        grid_spec=pltpu.PrefetchScalarGridSpec(
            num_scalar_prefetch=1,
            grid=(n,),
            in_specs=[
                pl.BlockSpec((tile, width), place),
                pl.BlockSpec((tile // NB, 1, NB), lambda g, o: place(g, o) + (0,)),
                pl.BlockSpec((1, 1, NB), lambda g, o: (rows // NB, 0, 0)),
                pl.BlockSpec((1, width), lambda g, o: (0, 0)),
                VMEM,
            ]
            + [ANY] * len(held),
            out_specs=[
                pl.BlockSpec((tile, width), place),
                pl.BlockSpec((1, tile, size), lambda g, o: (jnp.maximum(g - 2, 0), 0, 0)),
            ]
            + send_specs,
        ),
        out_shape=[
            jax.ShapeDtypeStruct((rows, width), BF16),
            jax.ShapeDtypeStruct((2, tile, size), F32),
        ]
        + sends,
        input_output_aliases={} if w is None else {6: 0},
        name="weigh_and_sketch",
        cost_estimate=cost(40 * n * tile * width * size, 6 * n * tile * width),
        compiler_params=limit(44),
    )(order, small, totals, totals, ctx_counts, omega, *held)


PACKED = (((0, 0), (0, 1), (0, 2), (0, 3), (3, 3)), ((1, 1), (1, 2), (1, 3), (2, 2), (2, 3)))


def gram_body(parts_of, core, *refs):
    n = sum(len(parts) for parts in parts_of)
    terms, (sketch, sketch_b, own, send) = refs[:n], refs[n : n + 4]
    held, arrival = refs[n + 4 : -1], refs[-1]
    which = [at for parts in parts_of for at in parts]
    copies = [
        pltpu.make_async_copy(terms[i] if at is None else terms[i].at[at], held[i], arrival.at[i])
        for i, at in enumerate(which)
    ]
    for copy in copies:
        copy.start()
    at, i = 0, 0
    for parts in parts_of:
        total = None
        for _ in parts:
            copies[i].wait()
            value = held[i][...].astype(F32)
            total = value if total is None else total + value
            i += 1
        sketch[at : at + total.shape[0], :] = total
        at += total.shape[0]
    sketch_b[...] = sketch[...].astype(BF16)
    size = sketch.shape[1] // 4
    col = lambda i, j: sketch[:, i * size : j * size]
    upper = lambda i, j: dot(col(i, i + 1), col(i, j), ROWS, HIGHEST)
    halves = [
        jnp.concatenate([upper(0, 4), upper(3, 4)], axis=1),
        jnp.concatenate([upper(1, 4), upper(2, 4)], axis=1),
    ]
    for which in range(2):

        @pl.when(core[0] == which)
        def _(which=which):
            own[...] = halves[which]
            send[...] = halves[1 - which]


def gram_of(core, pieces):
    terms = [array for piece in pieces for array, _ in piece]
    parts_of = [[which for _, which in piece] for piece in pieces]
    size = terms[0].shape[-1]
    rows = sum(piece[0][0].shape[-2] for piece in pieces)
    return pl.pallas_call(
        functools.partial(gram_body, parts_of),
        grid=(1,),
        in_specs=[SMEM] + [HBM] * len(terms),
        out_specs=[whole(rows, size)] * 2 + [whole(size // 4, size // 4 * 5)] * 2,
        out_shape=[
            jax.ShapeDtypeStruct((rows, size), F32),
            jax.ShapeDtypeStruct((rows, size), BF16),
            jax.ShapeDtypeStruct((size // 4, size // 4 * 5), F32),
            jax.ShapeDtypeStruct((size // 4, size // 4 * 5), F32),
        ],
        scratch_shapes=[pltpu.VMEM(x.shape[-2:], x.dtype) for x in terms]
        + [pltpu.SemaphoreType.DMA((len(terms),))],
        name="gram",
        cost_estimate=cost(12 * rows * size * size, 8 * rows * size),
        compiler_params=limit(60),
    )(core, *terms)


def small_factor(g):
    n = len(g)
    g = [list(r) for r in g]
    m = [[None] * n for _ in range(n)]
    pairs = []
    for j in range(0, n, 2):
        k = j + 1
        a, b, c = g[j][j], g[k][j], g[k][k]
        over = 1.0 / (a * c - b * b)
        ca, cb, cc = a * over, b * over, c * over
        pairs.append((a, ca, cb, cc))
        for i in range(k + 1, n):
            f = cc * g[i][j] - cb * g[i][k]
            h = ca * g[i][k] - cb * g[i][j]
            for l in range(k + 1, i + 1):
                g[i][l] = g[i][l] - (f * g[l][j] + h * g[l][k])
            for l in range(j):
                m[i][l] = m[i][l] - (f * m[j][l] + h * m[k][l])
            m[i][j], m[i][k] = -f, -h
    return m, pairs


def total(terms):
    while len(terms) > 1:
        terms = [x + y for x, y in zip(terms[::2], terms[1::2])] + terms[len(terms) // 2 * 2 :]
    return terms[0]


def eliminate(tiles, done):
    shape, n, group = tiles[0].shape, len(tiles), 2
    lane = lax.broadcasted_iota(jnp.int32, shape, 1)
    sub = lax.broadcasted_iota(jnp.int32, shape, 0)
    spread = lambda x: jnp.broadcast_to(x, shape)
    columns = lambda x: tuple(spread(x[:, m : m + 1]) for m in range(8))
    pivots = lane < 8

    def turn(t, carry):
        here, tiles = carry
        g = [[spread(here[l][i : i + 1]) for l in range(i + 1)] for i in range(8)]
        rows = [
            jnp.where(pivots, jnp.where(lane == k, 1.0, 0.0), spread(tiles[0][k : k + 1])) for k in range(8)
        ]
        m, pairs = small_factor(g)
        u = [total([rows[i]] + [m[i][l] * rows[l] for l in range(i // 2 * 2)]) for i in range(8)]
        v, y = [], []
        for j, (a, ca, cb, cc) in zip(range(0, 8, 2), pairs):
            v += [cc * u[j] - cb * u[j + 1], ca * u[j + 1] - cb * u[j]]
            y += [u[j] * lax.rsqrt(a), v[j + 1] * lax.rsqrt(ca)]
        z = [total([v[l]] + [m[i][l] * v[i] for i in range(l // 2 * 2 + 2, 8)]) for l in range(8)]
        new = []
        for x in tiles[1:]:
            x = jnp.where(pivots, 0.0, x) - total([c * w for c, w in zip(columns(x), z)])
            new.append(pltpu.roll(x, NB - 8, 1))
            if len(new) == 1:
                here = columns(new[0])
        final = y[0]
        for r in range(1, 8):
            final = jnp.where(sub == r, y[r], final)
        done[pl.ds(pl.multiple_of(8 * t, 8), 8), :] = final
        return here, tuple(new) + (jnp.zeros(shape, F32),)

    carry = columns(tiles[0]), tuple(tiles)
    for start in range(0, n, group):
        here, tiles = lax.fori_loop(start, start + group, turn, carry)
        carry = here, tiles[: n - start - group]
    return [done[0:8, :]] + [pltpu.roll(done[8 * t : 8 * t + 8, :], 8 * t, 1) for t in range(1, n)]


def factor_body(core, mine, other, out, halves, t, done):
    size = t.shape[0]
    n = size // NB
    block = lambda i: slice(i * NB, (i + 1) * NB)
    halves[core[0]] = mine[...]
    halves[1 - core[0]] = other[...]
    trace = jnp.float32(0.0)
    for half in range(2):
        for at, (i, j) in enumerate(PACKED[half]):
            value = halves[half, :, block(at)]
            t[block(i), block(j)] = value
            if i == j:
                trace = trace + jnp.sum(jnp.where(eye(NB), value, 0.0))
    amount = jnp.float32(0.0001) * trace / jnp.float32(size)
    lower = lax.broadcasted_iota(jnp.int32, (NB, NB), 1) <= lax.broadcasted_iota(jnp.int32, (NB, NB), 0)
    for p in range(n):
        here, before = block(p), slice(0, p * NB)
        diagonal = t[here, here] + jnp.where(eye(NB), amount, 0.0)
        tiles = eliminate([diagonal[8 * i : 8 * i + 8] for i in range(NB // 8)], done)
        inverse = jnp.where(lower, jnp.concatenate(tiles, 0), 0.0)
        out[here, here] = inverse
        if p:
            left = dot(inverse, t[here, before], ((1,), (0,)), HIGHEST)
            out[here, before] = left
        if p < n - 1:
            rest = slice((p + 1) * NB, size)
            out[here, rest] = jnp.zeros((NB, size - (p + 1) * NB), F32)
            right = dot(inverse, t[here, rest], ((1,), (0,)), HIGHEST)
            for q in range(p + 1, n):
                off = (q - p - 1) * NB
                use = right[:, off : off + NB]
                t[block(q), q * NB :] = t[block(q), q * NB :] - dot(use, right[:, off:], ROWS, HIGHEST)
                t[block(q), here] = -dot(use, inverse, ROWS, HIGHEST)
                if p:
                    t[block(q), before] = t[block(q), before] - dot(use, left, ROWS, HIGHEST)


def factor_inverse(core, mine, other):
    size = mine.shape[0] * 4
    return pl.pallas_call(
        factor_body,
        grid=(1,),
        in_specs=[SMEM, whole(*mine.shape), whole(*mine.shape)],
        out_specs=whole(size, size),
        out_shape=jax.ShapeDtypeStruct((size, size), F32),
        scratch_shapes=[
            pltpu.VMEM((2,) + mine.shape, F32),
            pltpu.VMEM((size, size), F32),
            pltpu.VMEM((NB, NB), F32),
        ],
        name="factor_inverse",
        cost_estimate=cost(1, 1),
        compiler_params=limit(24),
    )(core, mine, other)


def basis_body(inverse, sketch, *refs):
    refs[-1][...] = dot(sketch[...], inverse[...], COLS, HIGHEST)


def basis_of(inverse, sketch, tokens):
    rows, size = sketch.shape
    return pl.pallas_call(
        basis_body,
        grid=(1,),
        in_specs=[whole(size, size), whole(rows, size)] + [ANY] * len(tokens),
        out_specs=whole(rows, size),
        out_shape=jax.ShapeDtypeStruct((rows, size), F32),
        name="basis",
        cost_estimate=cost(1, 1),
        compiler_params=limit(24),
    )(inverse, sketch, *tokens)


def turned_body(n, place, inverse, *refs):
    shares, (turned, high, low) = refs[:n], refs[-3:]
    size = inverse.shape[0]
    quarter = size // 4
    step = pl.program_id(0)

    @pl.when(step == 0)
    def _():
        for i in range(4):
            rows = slice(i * quarter, (i + 1) * quarter)
            take = inverse[pl.ds(pl.multiple_of(place[i] * quarter, quarter), quarter), :]
            high[rows, :] = take.astype(BF16)
            low[rows, :] = (take - take.astype(BF16).astype(F32)).astype(BF16)

    for d in range(n):

        @pl.when(step == d)
        def _(d=d):
            value = dot(high[...], shares[d][...], COLS) + dot(low[...], shares[d][...], COLS)
            turned[...] = value.astype(BF16)


def turned_basis(place, inverse, shares, held, first, n_all, tokens):
    rows, size = shares[0].shape
    n = len(shares)
    held = ([] if held is None else [held]) + tokens
    return pl.pallas_call(
        functools.partial(turned_body, n),
        grid_spec=pltpu.PrefetchScalarGridSpec(
            num_scalar_prefetch=1,
            grid=(n,),
            in_specs=[whole(size, size)] + [whole(rows, size)] * n + [ANY] * len(held),
            out_specs=pl.BlockSpec((size, rows), lambda g, p: (0, p[4 + first + g])),
            scratch_shapes=[pltpu.VMEM((size, size), BF16)] * 2,
        ),
        out_shape=jax.ShapeDtypeStruct((size, n_all * rows), BF16),
        input_output_aliases={2 + n: 0} if first else {},
        name="turned_basis",
        cost_estimate=cost(4 * n * rows * size * size, 4 * n * rows * size),
        compiler_params=limit(24),
    )(place, inverse, *shares, *held)


def project_body(turned, w, *refs):
    send, own = refs[-2:]
    half = send.shape[0]
    value = jnp.dot(turned[...], w[...], preferred_element_type=F32)
    send[...] = value[:half].astype(BF16)
    own[...] = value[half:]


def project(turned, w, tokens, start, width, tile):
    size, rows = turned.shape
    steps = width // tile
    first = start // tile
    out = lambda g: (0, g)
    return pl.pallas_call(
        project_body,
        grid=(steps,),
        in_specs=[
            pl.BlockSpec((size, rows), lambda g: (0, 0), pipeline_mode=pl.Buffered(1)),
            pl.BlockSpec((rows, tile), lambda g: (0, first + g)),
        ]
        + [ANY] * len(tokens),
        out_specs=[pl.BlockSpec((size // 2, tile), out), pl.BlockSpec((size // 2, tile), out)],
        out_shape=[
            jax.ShapeDtypeStruct((size // 2, width), BF16),
            jax.ShapeDtypeStruct((size // 2, width), F32),
        ],
        name="project",
        cost_estimate=cost(40 * rows * size * width, 2 * rows * width),
        compiler_params=limit(34),
    )(turned, w, *tokens)


def finish_body(scale, start, mine, core_term, chip_term, *refs):
    out, tick, turned, arrival = refs[-4:]
    tick[...] = jnp.zeros_like(tick)
    total = mine[...] + core_term[...].astype(F32) + chip_term[...].astype(F32)
    turned[...] = jnp.transpose(total * scale)
    copy = pltpu.make_async_copy(turned, out.at[pl.ds(start, turned.shape[0])], arrival)
    copy.start()
    copy.wait()


def finish(own, core_term, chip_term, out, start, full, scale, tokens):
    size, width = chip_term.shape
    held = [] if out is None else [out]
    return pl.pallas_call(
        functools.partial(finish_body, scale, start),
        grid=(1,),
        in_specs=[
            pl.BlockSpec((size, width), lambda g: (1, 0)),
            pl.BlockSpec((size, width), lambda g: (1, 0)),
            whole(size, width),
        ]
        + [ANY] * len(held + tokens),
        out_specs=[ANY, whole(8, NB)],
        out_shape=[jax.ShapeDtypeStruct((full, size), F32), jax.ShapeDtypeStruct((8, NB), F32)],
        input_output_aliases={3: 0} if held else {},
        scratch_shapes=[pltpu.VMEM((width, size), F32), pltpu.SemaphoreType.DMA],
        name="finish",
        cost_estimate=cost(1, 1),
        compiler_params=limit(24),
    )(own, core_term, chip_term, *held, *tokens)


def pass_body(mine, core_term, *refs):
    refs[-1][...] = (mine[...] + core_term[...].astype(F32)).astype(BF16)


def pass_on(own, core_term, tokens):
    size, width = own.shape[0] // 2, own.shape[1]
    return pl.pallas_call(
        pass_body,
        grid=(1,),
        in_specs=[whole(size, width), whole(size, width)] + [ANY] * len(tokens),
        out_specs=whole(size, width),
        out_shape=jax.ShapeDtypeStruct((size, width), BF16),
        name="pass_on",
        cost_estimate=cost(1, 1),
        compiler_params=limit(24),
    )(own, core_term, *tokens)


def rotate(x, n, by):
    return lax.ppermute(x, "col", [(i, (i + by) % n) for i in range(n)])


def swap_col(x, bit):
    return lax.ppermute(x, "col", [(i, i ^ bit) for i in range(4)])


def swap(x, bit):
    return lax.ppermute(x, "row", [(i, i ^ bit) for i in range(4)])


def half_of(x, which):
    rows = x.shape[0] // 2
    return lax.dynamic_slice_in_dim(x, which * rows, rows, 0)


def stack_by(which, mine, other):
    return jnp.where(which == 0, jnp.concatenate([mine, other]), jnp.concatenate([other, mine]))


def pieces_of(share):
    n = share // NB
    return [2 * NB] * ((n - 2) // 2) + [NB] * (n - (n - 2) // 2 * 2) if n > 2 else [NB] * n


def sketch_phase(counts, ctx_counts, omega, col):
    rows, width = counts.shape
    ctx_counts = ctx_counts.reshape(1, width)
    totals, small = row_sums(counts, ctx_counts)
    totals = totals + swap_col(totals, 1)
    totals = totals + swap_col(totals, 2)
    order = jnp.stack([col ^ 1, col ^ 3, col ^ 2, col])
    tiles = pieces_of(rows // 4)
    w, offset, pieces, passed, arrived = None, 0, [], [], []
    for k, tile in enumerate(tiles):
        last = k == len(tiles) - 1
        tokens = passed[k - 2 : k - 1] if k >= 2 else []
        tokens = tokens + (arrived[k - 3 : k - 2] if k >= 3 else [])
        w, keep, *sends = weigh(small, totals, ctx_counts, omega, w, order, offset, tile, tokens, last)
        offset += tile
        if last:
            theirs, mine = swap_col(sends[1], 1), swap_col(sends[0], 1)
            passed.append(pass_on(keep.reshape(2 * tile, -1), theirs, arrived[: max(0, k - 1)]))
            mine = (mine, None)
        else:
            near = swap_col(sends[0], 1)
            passed.append((keep[0] + near[1].astype(F32)).astype(BF16))
            mine = (near, 0)
        arrived.append(swap_col(passed[k], 2))
        pieces.append([(keep, 1), mine, (arrived[k], None)])
    return w, pieces


def sketch_phase_any(counts, ctx_counts, omega, col):
    row_part = jnp.sum(counts.astype(F32), axis=1)
    ctx_weight = ctx_counts.astype(F32) ** 0.75
    log_ctx = jnp.log(ctx_weight)[None, :]
    row_total, ctx_total = lax.psum((row_part, jnp.sum(ctx_weight)), "col")
    value = jnp.log(counts.astype(F32)) + (
        jnp.log(ctx_total) - jnp.log(F32(5.0)) - jnp.log(row_total)[:, None] - log_ctx
    )
    w = jnp.maximum(value, 0.0).astype(BF16)
    partial = jnp.dot(w, omega, preferred_element_type=F32)
    return w, [[(lax.psum_scatter(partial, "col", scatter_dimension=0, tiled=True), None)]]


def shards(counts, ctx_counts, omega):
    rows, width = counts.shape
    n = lax.axis_size("col")
    row = lax.axis_index("row")
    col = lax.axis_index("col")
    core, chip = row % 2, row // 2
    direct = n == 4 and rows % (4 * NB) == 0
    phase = sketch_phase if direct else sketch_phase_any
    w, pieces = phase(counts, ctx_counts, omega, col)
    sketch, sketch_b, half, other_half = gram_of(core.reshape(1), pieces)
    half = half + swap(other_half, 1)
    quarter = half_of(half, chip) + swap(half_of(half, 1 - chip), 2)
    if direct:
        quarter = quarter + swap_col(quarter, 1)
        quarter = quarter + swap_col(quarter, 2)
        shares = [sketch_b] + [rotate(sketch_b, n, d) for d in (1, 2, 3)]
        sources = [(col - d) % n for d in range(n)]
    else:
        quarter = lax.psum(quarter, "col")
        shares = [lax.all_gather(sketch_b, "col", tiled=True)]
        sources = [jnp.int32(0)]
    half = stack_by(chip, quarter, swap(quarter, 2))
    inverse = factor_inverse(core.reshape(1), half, swap(half, 1))
    place = jnp.stack([row ^ 3, row ^ 1, row ^ 2, row] + sources)
    n_share = len(shares)
    first = (n_share + 1) // 2
    turned = turned_basis(place, inverse, shares[:first], None, 0, n_share, [])
    basis = basis_of(inverse, sketch, [])
    if n_share > 1:
        turned = turned_basis(place, inverse, shares[first:], turned, first, n_share, [basis])
    widths = (1, 2, 3, 3, 4, 2, 1) if width % (16 * NB) == 0 else (1,) * 8
    unit = width // sum(widths)
    scale = float(1.0 / (rows * lax.axis_size("row")) ** 0.5)
    quarter = omega.shape[1] // 4
    out, start = None, 0
    sent, passed, arrived, ended = [], [], [], []
    terms = []

    def end(tokens):
        j = len(ended)
        out = ended[-1][0] if ended else None
        ended.append(finish(*terms[j][:2], arrived[j], out, terms[j][2], width, scale, tokens))

    for j, pieces in enumerate(widths):
        piece = pieces * unit
        tokens = sent[-1:] + (passed[-2:-1] if j >= 2 else []) + (arrived[-3:-2] if j >= 3 else [])
        send, mine = project(turned, w, tokens, start, piece, unit)
        sent.append(send)
        core_term = swap(send, 1)
        if j == len(widths) - 1:
            for _ in range(3):
                end([])
            chip_send = pass_on(mine, core_term, [arrived[-2], ended[-1][1]])
        else:
            chip_send = (mine[:quarter] + core_term[:quarter].astype(F32)).astype(BF16)
        passed.append(chip_send)
        arrived.append(swap(chip_send, 2))
        terms.append((mine, core_term, start))
        start += piece
    while len(ended) < len(widths):
        end([])
    out = ended[-1][0]
    return (basis, out)


def solution(mesh):
    in_specs = (P(("grp", "row"), "col"), P(("grp", "col")), P("col", None))
    out_specs = (P(("grp", "row", "col"), None), P(("grp", "col"), "row"))
    return jax.shard_map(shards, mesh=mesh, in_specs=in_specs, out_specs=out_specs, check_vma=False)
```
